512 devices in a mesh: ctx: 8 (over y, x_hi), tp: 32 (over z, core), store: 2 (over x_lo).
Axes of the slice: x: 4 (x_hi: 2, x_lo: 2; x = x_hi * 2 + x_lo), y: 4, z: 16, core: 2. Of those that a mesh axis runs over, the one named last changes fastest.
Arguments:
- query_nope: bfloat16 [4, 1024, 16384], P(None, 'ctx', ('tp', 'store')), may hold values from -4.5 to 4.5
- query_rope: bfloat16 [4, 1024, 8192], P(None, 'ctx', ('tp', 'store')), may hold values from -400 to 400
- key_up: bfloat16 [128, 128, 512], P(('tp', 'store')), may hold values from -0.5 to 0.5
- value_up: bfloat16 [128, 512, 128], P(('tp', 'store')), may hold values from -6 to 6
- new_latent: bfloat16 [4, 1024, 512], P(None, 'ctx'), may hold values from -6 to 6
- new_rope: bfloat16 [4, 1024, 64], P(None, 'ctx'), may hold values from -6 to 6
- cache_latent: bfloat16 [512, 64, 512], P(('ctx', 'store')), may hold values from -6 to 6
- cache_rope: bfloat16 [512, 64, 64], P(('ctx', 'store')), may hold values from -6 to 6
- block_owner: int32 [4, 24], replicated, may hold values from 0 to 15, as said below
- block_slot: int32 [4, 24], replicated, may hold values from 0 to 31
- cached_len: int32 [4], replicated, may hold values from 1 to 1536, as said below
Outputs:
- attended: bfloat16 [4, 1024, 16384], P(None, 'ctx', ('tp', 'store'))
The draws below stay inside these ranges and needn't reach their ends.
Inputs may be any that keep to these rules, and one draw needn't show every extreme that they name: block_owner[s, j] is the holder (index over ctx, then store) of block j of sequence s; no two table entries name the same pool block; a holder holds at most 9 blocks named in the tables, and some holder exactly 9. `cached_len`: some sequence has exactly 1536 cached tokens.
All inputs are finite; a program needn't handle non-finite values.
Results may differ from the reference program's by a relative error of at most 0.008.
Values may be sent and summed in bfloat16 or wider, within the bound.
No kernel may reach another device: no remote copies, remote signals or barrier semaphores. Data moves between devices by JAX's collectives and lax.ppermute only.
A program may use at most 128 MiB of HBM per device.

```python
import jax
import jax.numpy as jnp
from jax import lax

L = 512
RO = 64
NOPE = 128
VH = 128
H = 128
SEQS = 4
NEW = 1024
BT = 64
MAXBLK = 24
MAXLEN = 1536
HOLDERS = 16
POOL_DEV = 32
POOL = 512
CAP = 9


def table_base(key):
    spots = HOLDERS * CAP
    listed = SEQS * MAXBLK
    key_hot, key_order, key_shuffle, key_slots = jax.random.split(key, 4)
    hottest = jax.random.randint(key_hot, (), 0, HOLDERS)
    order = jax.random.permutation(key_order, spots)
    holder_of = jnp.arange(spots) // CAP
    priority = order + jnp.where(holder_of == hottest, spots, 0)
    ranked, chosen = lax.top_k(priority, listed)
    shuffled = chosen[jax.random.permutation(key_shuffle, listed)]
    owners = shuffled // CAP
    slot_keys = jax.random.split(key_slots, HOLDERS)

    def slot_order(single_key):
        return jax.random.permutation(single_key, POOL_DEV)
    slot_orders = jax.vmap(slot_order)(slot_keys)
    slots = slot_orders[owners, shuffled % CAP]
    return (owners.reshape(SEQS, MAXBLK).astype(jnp.int32), slots.reshape(SEQS, MAXBLK).astype(jnp.int32))


def draw_block_owner(key, part):
    return table_base(key)[0]


def draw_block_slot(key, part):
    return table_base(key)[1]


def draw_cached_len(key, part):
    key = jax.random.fold_in(key, 7)
    key_len, key_top = jax.random.split(key)
    lengths = jax.random.randint(key_len, (SEQS,), 1, MAXLEN + 1)
    longest = jax.random.randint(key_top, (), 0, SEQS)
    return jnp.where(jnp.arange(SEQS) == longest, MAXLEN, lengths).astype(jnp.int32)


def rope_base(key):
    return jnp.clip(jax.random.normal(key, (SEQS, NEW, RO), jnp.float32), -6.0, 6.0)


def draw_new_rope(key, part):
    values = rope_base(key)
    return values.astype(jnp.bfloat16)


def draw_query_rope(key, part):
    key = jax.random.fold_in(key, 13)
    values = jnp.clip(jax.random.normal(key, (SEQS, NEW, H * RO), jnp.float32), -6.0, 6.0)
    return values.astype(jnp.bfloat16)


def steps_of(rng, shape, shards, low, largest):
    factor_of, own = 1.0, jax.random.fold_in(rng, 6)
    for position, shards_of in shards:
        heights = jnp.exp(jax.random.uniform(jax.random.fold_in(own, position), (shards_of,), jnp.float32, low / len(shards), largest / len(shards)))
        factor_of = factor_of * jnp.repeat(heights, shape[position] // shards_of).reshape([-1 if axis == position else 1 for axis in range(len(shape))])
    return factor_of


def centred(key, extent, spread, bound, shards=(), kind=jnp.bfloat16):
    values = jax.random.normal(key, extent, jnp.float32) * spread
    if len(shards) > 0:
        values = steps_of(key, extent, shards, -0.22, 0.18) * values
    return jnp.clip(values, min=-bound, max=bound).astype(kind)


def setup_inputs(seed: int = 0) -> dict:
    arg_keys = jax.random.split(jax.random.key(seed), 12)
    return {
        "query_nope": centred(arg_keys[0], (SEQS, NEW, H * NOPE), 0.7, 4.5, ((1, 8), (2, 64))),
        "query_rope": draw_query_rope(jax.random.fold_in(arg_keys[11], 71), 0),
        "key_up": centred(arg_keys[2], (H, NOPE, L), NOPE ** -0.5, 0.5, ((0, 64),)),
        "value_up": centred(arg_keys[3], (H, L, VH), 1.0, 6.0, ((0, 64),)),
        "new_latent": centred(arg_keys[4], (SEQS, NEW, L), 1.0, 6.0, ((1, 8),)),
        "new_rope": draw_new_rope(jax.random.fold_in(arg_keys[11], 71), 0),
        "cache_latent": centred(arg_keys[6], (POOL, BT, L), 1.0, 6.0, ((0, 16),)),
        "cache_rope": centred(arg_keys[7], (POOL, BT, RO), 1.0, 6.0, ((0, 16),)),
        "block_owner": draw_block_owner(jax.random.fold_in(arg_keys[11], 71), 0),
        "block_slot": draw_block_slot(jax.random.fold_in(arg_keys[11], 71), 0),
        "cached_len": draw_cached_len(jax.random.fold_in(arg_keys[11], 71), 0),
    }


NEG = -1e30
score_scale = 192.0 ** -0.5


def reference(query_nope, query_rope, key_up, value_up, new_latent, new_rope, cache_latent, cache_rope, block_owner, block_slot, cached_len):
    heads = key_up.shape[0]
    split_nope = query_nope.reshape(SEQS, NEW, heads, NOPE).astype(jnp.float32)
    query_latent = jnp.einsum('sthn,hnl->hstl', split_nope, key_up.astype(jnp.float32)).astype(jnp.bfloat16)
    query_pos = query_rope.reshape(SEQS, NEW, heads, RO).transpose(2, 0, 1, 3)
    index = (block_owner * POOL_DEV + block_slot).astype(jnp.int32)
    old_latent = cache_latent[index].reshape(SEQS, MAXLEN, L)
    old_rope = cache_rope[index].reshape(SEQS, MAXLEN, RO)
    keys_latent = jnp.concatenate([old_latent, new_latent], 1).astype(jnp.float32)
    keys_rope = jnp.concatenate([old_rope, new_rope], 1).astype(jnp.float32)
    old_live = jnp.arange(MAXLEN)[None, :] < cached_len[:, None]
    new_live = jnp.arange(NEW)[None, :] <= jnp.arange(NEW)[:, None]
    live = jnp.concatenate([jnp.broadcast_to(old_live[:, None, :], (SEQS, NEW, MAXLEN)),
                            jnp.broadcast_to(new_live[None], (SEQS, NEW, NEW))], -1)

    def one_head(inputs):
        head_latent, head_pos, head_value = inputs
        scores = jnp.einsum('stl,skl->stk', head_latent.astype(jnp.float32), keys_latent)
        scores = (scores + jnp.einsum('std,skd->stk', head_pos.astype(jnp.float32), keys_rope)) * score_scale
        scores = jnp.where(live, scores, NEG)
        highest = jnp.max(scores, -1, keepdims=True)
        expo = jnp.where(live, jnp.exp(scores - highest), 0.0)
        denom = jnp.sum(expo, -1, keepdims=True)
        weights = lax.optimization_barrier(expo.astype(jnp.bfloat16)).astype(jnp.float32)
        mixed = (jnp.einsum('stk,skl->stl', weights, keys_latent) / denom).astype(jnp.bfloat16)
        result = jnp.dot(mixed.reshape(SEQS * NEW, L), head_value, preferred_element_type=jnp.float32)
        return result.reshape(SEQS, NEW, VH).astype(jnp.bfloat16)

    outputs = lax.map(one_head, (query_latent, query_pos, value_up))
    return outputs.transpose(1, 2, 0, 3).reshape(SEQS, NEW, heads * VH)
```

```python
import functools

import jax
import jax.numpy as jnp
from jax import lax
from jax.experimental import pallas as pl
from jax.experimental.pallas import tpu as pltpu
from jax.sharding import Mesh
from jax.sharding import PartitionSpec as P

NEG = -1e30
LOG2E = 1.4426950408889634
EXP_SCALE = 192.0 ** (-0.5) * LOG2E
PLANE = ("y", "xh", "xl")
ROW = ("xh", "xl")
CAP = 9
PIECE = 16
HALF = 256
WIDE = 384
VMEM_LIMIT = 50 * 1024 * 1024


def pack_kernel(
    info,
    owner,
    slot,
    cache_latent,
    cache_rope,
    new_latent,
    new_rope,
    out,
    slots,
    lat,
    rope,
    nlat,
    nrope,
    sems,
):
    holder = info[0]
    core = info[1]
    xl = info[2]
    cols = pl.ds(pl.multiple_of(core * HALF, HALF), HALF)
    rows = pl.ds(pl.multiple_of(xl * 64, 64), 64)
    copies = [
        pltpu.make_async_copy(new_latent.at[:, rows, cols], nlat, sems.at[0]),
        pltpu.make_async_copy(new_rope.at[:, rows, :], nrope, sems.at[1]),
    ]
    for c in copies:
        c.start()
    for r in range(CAP):
        slots[r] = 0

    def scan(e, count):
        hit = owner[e] == holder

        @pl.when(hit & (count < CAP))
        def _():
            slots[count] = slot[e]

        return count + hit.astype(jnp.int32)

    lax.fori_loop(0, owner.shape[0], scan, jnp.int32(0))
    block_copies = []
    for r in range(CAP):
        a = pltpu.make_async_copy(cache_latent.at[slots[r], :, cols], lat.at[r], sems.at[2 + 2 * r])
        b = pltpu.make_async_copy(cache_rope.at[slots[r]], rope.at[r], sems.at[3 + 2 * r])
        a.start()
        b.start()
        block_copies.append((a, b))
    for c in copies:
        c.wait()
    pad = jnp.zeros((64, 64), jnp.bfloat16)
    for s in range(4):
        piece = jnp.concatenate([nlat[s], nrope[s], pad], axis=1)
        for x in range(4):
            out[s * 4 + x, CAP * PIECE :, :] = piece
    for r in range(CAP):
        for c in block_copies[r]:
            c.wait()
        whole = jnp.concatenate([lat[r], rope[r], pad], axis=1)
        for x in range(4):
            piece = whole[x * PIECE : (x + 1) * PIECE]
            for s in range(4):
                out[s * 4 + x, r * PIECE : (r + 1) * PIECE, :] = piece


def select_kernel(info, owner, recv, out, new_out, counts, sel, nbuf, sems):
    seq = info[3]
    per = owner.shape[0] // 4
    new_in = pltpu.make_async_copy(recv.at[:, CAP * PIECE :, :], nbuf, sems.at[per])
    new_in.start()
    for h in range(16):
        counts[h] = 0

    def scan(e, carry):
        h = owner[e]
        counts[h] = counts[h] + 1
        return carry

    lax.fori_loop(0, seq * per, scan, jnp.int32(0))
    copies = []
    for j in range(per):
        h = owner[seq * per + j]
        rank = jnp.minimum(counts[h], CAP - 1)
        counts[h] = counts[h] + 1
        c = pltpu.make_async_copy(
            recv.at[h, pl.ds(pl.multiple_of(rank * PIECE, PIECE), PIECE), :],
            sel.at[pl.ds(j * PIECE, PIECE), :],
            sems.at[j],
        )
        c.start()
        copies.append(c)
    for c in copies:
        c.wait()
    for x in range(4):
        out[x] = sel[...]
    new_in.wait()
    new_out[...] = nbuf[...]


def dot(a, b):
    return lax.dot_general(a, b, (((1,), (0,)), ((), ())), preferred_element_type=jnp.float32)


def dot_t(a, b):
    return lax.dot_general(a, b, (((1,), (1,)), ((), ())), preferred_element_type=jnp.float32)


def attend_kernel(
    info,
    cached_len,
    query,
    key_up,
    value_up,
    cache_own,
    cache_other,
    new_own,
    new_other,
    out,
    keys,
    sems,
):
    core = info[1]
    xh = info[4]
    seq = info[3]
    old = cache_own.shape[0]
    new = new_own.shape[0]
    own_cols = pl.ds(pl.multiple_of(core * HALF, HALF), HALF)
    other_cols = pl.ds(pl.multiple_of((1 - core) * HALF, HALF), HALF)
    copies = []
    for i, (own, other, start, count) in enumerate(
        ((cache_own, cache_other, 0, old), (new_own, new_other, old, new))
    ):
        rows = pl.ds(start, count)
        copies += [
            pltpu.make_async_copy(own.at[:, pl.ds(0, HALF)], keys.at[rows, own_cols], sems.at[3 * i]),
            pltpu.make_async_copy(
                other.at[:, pl.ds(0, HALF)], keys.at[rows, other_cols], sems.at[3 * i + 1]
            ),
            pltpu.make_async_copy(
                own.at[:, pl.ds(HALF, 128)], keys.at[rows, pl.ds(2 * HALF, 128)], sems.at[3 * i + 2]
            ),
        ]
    for c in copies:
        c.start()
    index = lax.broadcasted_iota(jnp.int32, (1, old), 1)
    per_x = old // 4
    rest = index % per_x
    position = (rest // PIECE) * (4 * PIECE) + (index // per_x) * PIECE + rest % PIECE
    bias = jnp.where(position < cached_len[seq], 0.0, NEG).astype(jnp.float32)
    tok = query.shape[1]
    row_tok = lax.broadcasted_iota(jnp.int32, (2 * tok, 2 * tok), 0) % tok + xh * tok
    col = lax.broadcasted_iota(jnp.int32, (2 * tok, 2 * tok), 1)
    causal = jnp.where(col <= row_tok, 0.0, NEG).astype(jnp.float32)
    pad = jnp.zeros((tok, 64), jnp.bfloat16)
    joint = []
    for chunk in range(4):
        parts = []
        for h in range(2):
            latent = dot(query[chunk, :, h * 128 : (h + 1) * 128], key_up[h]).astype(jnp.bfloat16)
            pos = query[chunk, :, 256 + h * 64 : 256 + (h + 1) * 64]
            parts.append(jnp.concatenate([latent, pos, pad], axis=1))
        joint.append(jnp.concatenate(parts, axis=0))
    for c in copies:
        c.wait()
    for chunk in range(4):
        q = joint[chunk]
        full = old + chunk * 2 * tok
        pieces = [dot_t(q, keys[0:old, :]) + bias]
        if chunk:
            pieces.append(dot_t(q, keys[old:full, :]))
        pieces.append(dot_t(q, keys[full : full + 2 * tok, :]) + causal)
        top = functools.reduce(jnp.maximum, [jnp.max(p, -1, keepdims=True) for p in pieces])
        expo = [jnp.exp2((p - top) * EXP_SCALE) for p in pieces]
        denom = functools.reduce(jnp.add, [jnp.sum(e, -1, keepdims=True) for e in expo])
        weights = [e.astype(jnp.bfloat16) for e in expo]
        total = dot(weights[0], keys[0:old, 0:512])
        if chunk:
            total += dot(weights[1], keys[old:full, 0:512])
        total += dot(weights[-1], keys[full : full + 2 * tok, 0:512])
        mixed = (total / denom).astype(jnp.bfloat16)
        for h in range(2):
            out[chunk, :, h * 128 : (h + 1) * 128] = dot(
                mixed[h * tok : (h + 1) * tok], value_up[h]
            ).astype(jnp.bfloat16)


def smem():
    return pl.BlockSpec(memory_space=pltpu.SMEM)


def vmem():
    return pl.BlockSpec(memory_space=pltpu.VMEM)


def hbm():
    return pl.BlockSpec(memory_space=pl.ANY)


def params():
    return pltpu.CompilerParams(vmem_limit_bytes=VMEM_LIMIT)


def on_device(
    query_nope,
    query_rope,
    key_up,
    value_up,
    new_latent,
    new_rope,
    cache_latent,
    cache_rope,
    block_owner,
    block_slot,
    cached_len,
):
    y = lax.axis_index("y")
    x = lax.axis_index(ROW)
    info = jnp.stack(
        [y * 4 + x, lax.axis_index("core"), lax.axis_index("xl"), y, lax.axis_index("xh")]
    ).astype(jnp.int32)
    owner = block_owner.reshape(-1)
    slot = block_slot.reshape(-1)
    entries = owner.shape[0] // 4
    chunk_rows = CAP * PIECE + 64
    bf16 = jnp.bfloat16

    send = pl.pallas_call(
        pack_kernel,
        out_shape=jax.ShapeDtypeStruct((16, chunk_rows, WIDE), bf16),
        in_specs=[smem(), smem(), smem(), hbm(), hbm(), hbm(), hbm()],
        out_specs=vmem(),
        scratch_shapes=[
            pltpu.SMEM((16,), jnp.int32),
            pltpu.VMEM((CAP, 64, HALF), bf16),
            pltpu.VMEM((CAP, 64, 64), bf16),
            pltpu.VMEM((4, 64, HALF), bf16),
            pltpu.VMEM((4, 64, 64), bf16),
            pltpu.SemaphoreType.DMA((2 + 2 * CAP,)),
        ],
        compiler_params=params(),
        name="pack",
    )(info, owner, slot, cache_latent, cache_rope, new_latent, new_rope)
    recv = lax.all_to_all(send, PLANE, 0, 0)

    query = jnp.concatenate([query_nope, query_rope], -1)
    query = lax.all_to_all(query, "y", 0, 0)

    picked, new_own = pl.pallas_call(
        select_kernel,
        out_shape=(
            jax.ShapeDtypeStruct((4, entries * PIECE, WIDE), bf16),
            jax.ShapeDtypeStruct((16, 64, WIDE), bf16),
        ),
        in_specs=[smem(), smem(), hbm()],
        out_specs=(vmem(), vmem()),
        scratch_shapes=[
            pltpu.SMEM((16,), jnp.int32),
            pltpu.VMEM((entries * PIECE, WIDE), bf16),
            pltpu.VMEM((16, 64, WIDE), bf16),
            pltpu.SemaphoreType.DMA((entries + 1,)),
        ],
        compiler_params=params(),
        name="select",
    )(info, owner, recv)
    swap = [(0, 1), (1, 0)]
    new_own = new_own.reshape(16 * 64, WIDE)
    new_other = lax.ppermute(new_own, "core", swap)
    cache_own = lax.all_to_all(picked, ROW, 0, 0).reshape(4 * entries * PIECE, WIDE)
    cache_other = lax.ppermute(cache_own, "core", swap)

    mixed = pl.pallas_call(
        attend_kernel,
        out_shape=jax.ShapeDtypeStruct((4, 128, 256), bf16),
        in_specs=[smem(), smem(), vmem(), vmem(), vmem(), hbm(), hbm(), hbm(), hbm()],
        out_specs=vmem(),
        scratch_shapes=[
            pltpu.VMEM((4 * entries * PIECE + 16 * 64, 640), bf16),
            pltpu.SemaphoreType.DMA((6,)),
        ],
        compiler_params=params(),
        name="attend",
    )(info, cached_len, query, key_up, value_up, cache_own, cache_other, new_own, new_other)
    return lax.all_to_all(mixed, "y", 0, 0)


def solution(mesh):
    fine = Mesh(mesh.devices.reshape(4, 2, 16, 2, 2), ("y", "xh", "z", "core", "xl"))
    ctx = ("y", "xh")
    heads = ("z", "core", "xl")
    holders = ("y", "xh", "xl")
    return jax.shard_map(
        on_device,
        mesh=fine,
        in_specs=(
            P(None, ctx, heads),
            P(None, ctx, heads),
            P(heads, None, None),
            P(heads, None, None),
            P(None, ctx, None),
            P(None, ctx, None),
            P(holders, None, None),
            P(holders, None, None),
            P(),
            P(),
            P(),
        ),
        out_specs=P(None, ctx, heads),
        check_vma=False,
    )
```

```python
import functools

import jax
import jax.numpy as jnp
from jax import lax
from jax.experimental import pallas as pl
from jax.experimental.pallas import tpu as pltpu
from jax.sharding import Mesh
from jax.sharding import PartitionSpec as P

NEG = -1e30
LOG2E = 1.4426950408889634
EXP_SCALE = 192.0 ** (-0.5) * LOG2E
PLANE = ("y", "xh", "xl")
SPREAD = ("xh", "zp", "xl")
CAP = 9
PIECE = 16
LANES = 128
SEQS = 4
BLOCKS = 24
TOK = 128
LAT_ROWS = CAP * PIECE
ROPE_ROWS = (CAP + 1) // 2 * PIECE
NEW_AT = LAT_ROWS + ROPE_ROWS
NEW_ROWS = 2 * 64 + 16
MSG_ROWS = NEW_AT + NEW_ROWS
PICK_LAT = BLOCKS * PIECE
PICK_PART = BLOCKS // 2 * PIECE // 4
PICK_ROWS = PICK_LAT + PICK_PART
MIB = 1024 * 1024
bf16 = jnp.bfloat16
f32 = jnp.float32


def coords(*names):
    return [lax.axis_index(n) for n in names]


def pack_kernel(
    owner,
    slot,
    cache_latent,
    cache_rope,
    new_latent,
    new_rope,
    out,
    owners,
    places,
    slots,
    lat,
    rope,
    nlat,
    nrope_t,
    nrope,
    cached_part,
    new_part,
    sems,
    out_sems,
):
    holder, core, xl, zp = coords(PLANE, "core", "xl", "zp")
    table_copies = [
        pltpu.make_async_copy(owner, owners, sems.at[2 + 2 * CAP]),
        pltpu.make_async_copy(slot, places, sems.at[3 + 2 * CAP]),
    ]
    for c in table_copies:
        c.start()
    cols = pl.ds(pl.multiple_of((core * 2 + zp) * LANES, LANES), LANES)
    half = pl.ds(pl.multiple_of(core * 2 * LANES, 2 * LANES), 2 * LANES)
    rows = pl.ds(pl.multiple_of(xl * 64, 64), 64)
    new_copies = [
        pltpu.make_async_copy(new_latent.at[:, rows, half], nlat, sems.at[0]),
        pltpu.make_async_copy(new_rope, nrope_t, sems.at[1]),
    ]
    for c in new_copies:
        c.start()
    for r in range(CAP):
        slots[r] = 0
    for c in table_copies:
        c.wait()
    count = jnp.int32(0)
    for s in range(SEQS):
        for j in range(BLOCKS):
            hit = owners[s, j] == holder
            slots[jnp.where(hit, jnp.minimum(count, CAP), CAP)] = places[s, j]
            count = count + hit.astype(jnp.int32)
    lat_copies, rope_copies = [], []
    for r in range(CAP):
        at = slots[r]
        lat_copies.append(pltpu.make_async_copy(cache_latent.at[at, :, cols], lat.at[r], sems.at[2 + 2 * r]))
        rope_copies.append(pltpu.make_async_copy(cache_rope.at[at], rope.at[r], sems.at[3 + 2 * r]))
        lat_copies[-1].start()
        rope_copies[-1].start()
    for c in new_copies:
        c.wait()
    low = pl.ds(pl.multiple_of(xl * 64 + core * 16, 16), 16)
    high = pl.ds(pl.multiple_of(xl * 64 + 32 + core * 16, 16), 16)
    for s in range(SEQS):
        nrope[s] = nrope_t[s].T
        new_part[s, 0:64, :] = nlat[s, :, 0:LANES]
        new_part[s, 64:128, :] = nlat[s, :, LANES : 2 * LANES]
        new_part[s, 128:144, :] = jnp.concatenate([nrope[s, low, :], nrope[s, high, :]], axis=1)
    out_copies = [
        pltpu.make_async_copy(new_part, out.at[:, x, pl.ds(NEW_AT, NEW_ROWS), :], out_sems.at[x])
        for x in range(4)
    ]
    for c in out_copies:
        c.start()
    for r in range(CAP):
        lat_copies[r].wait()
        for x in range(4):
            cached_part[x, r * PIECE : (r + 1) * PIECE, :] = lat[r, x * PIECE : (x + 1) * PIECE, :]
    for c in rope_copies:
        c.wait()
    for m in range((CAP + 1) // 2):
        first = rope[2 * m]
        second = rope[2 * m + 1] if 2 * m + 1 < CAP else first
        both = jnp.concatenate([first, second], axis=1)
        for x in range(4):
            cached_part[x, LAT_ROWS + m * PIECE : LAT_ROWS + (m + 1) * PIECE, :] = both[
                x * PIECE : (x + 1) * PIECE, :
            ]
    for s in range(SEQS):
        c = pltpu.make_async_copy(cached_part, out.at[s, :, pl.ds(0, NEW_AT), :], out_sems.at[4 + s])
        c.start()
        out_copies.append(c)
    for c in out_copies:
        c.wait()


def plan_kernel(owner, plan, counts):
    (seq,) = coords("y")
    for h in range(16):
        counts[h] = 0

    def scan(e, carry):
        h = owner[e // BLOCKS, e % BLOCKS]
        counts[h] = counts[h] + 1
        return carry

    lax.fori_loop(0, seq * BLOCKS, scan, jnp.int32(0))
    for j in range(BLOCKS):
        h = owner[seq, j]
        rank = jnp.minimum(counts[h], CAP - 1)
        counts[h] = counts[h] + 1
        plan[0, j] = h
        plan[1, j] = rank


def select_kernel(plan, recv, out, new_out, lat, tiles, pairs, nbuf, sems):
    core, zp = coords("core", "zp")
    copies = []
    for j in range(BLOCKS):
        h, rank = plan[0, j], plan[1, j]
        b = pltpu.make_async_copy(
            recv.at[h, pl.ds(pl.multiple_of(LAT_ROWS + rank // 2 * PIECE, PIECE), PIECE), :],
            tiles.at[j],
            sems.at[2 * j + 1],
        )
        b.start()
        copies.append(b)
    for j in range(BLOCKS):
        h, rank = plan[0, j], plan[1, j]
        a = pltpu.make_async_copy(
            recv.at[h, pl.ds(pl.multiple_of(rank * PIECE, PIECE), PIECE), :],
            lat.at[pl.ds(j * PIECE, PIECE), :],
            sems.at[2 * j],
        )
        a.start()
        copies.append(a)
    new_in = pltpu.make_async_copy(recv.at[:, pl.ds(NEW_AT, NEW_ROWS), :], nbuf, sems.at[2 * BLOCKS])
    new_in.start()
    for c in copies[:BLOCKS]:
        c.wait()
    for j in range(BLOCKS // 2):
        k = j + BLOCKS // 2
        first = jnp.where(plan[1, j] % 2 == 1, tiles[j, :, 64:128], tiles[j, :, 0:64])
        second = jnp.where(plan[1, k] % 2 == 1, tiles[k, :, 64:128], tiles[k, :, 0:64])
        pairs[j * PIECE : (j + 1) * PIECE, :] = jnp.concatenate([first, second], axis=1)
    part = pairs[pl.ds(pl.multiple_of((core * 2 + zp) * PICK_PART, 16), PICK_PART), :]
    for d in range(8):
        out[d, PICK_LAT:PICK_ROWS, :] = part
    for c in copies[BLOCKS:]:
        c.wait()
    for d in range(8):
        out[d, 0:PICK_LAT, :] = lat[...]
    new_in.wait()
    new_out[...] = nbuf[...]


def dot(a, b):
    return lax.dot_general(a, b, (((1,), (0,)), ((), ())), preferred_element_type=f32)


def dot_t(a, b):
    return lax.dot_general(a, b, (((1,), (1,)), ((), ())), preferred_element_type=f32)


def gather_query(refs, query, sems):
    (y,) = coords("y")
    copies = []
    for k in range(4):
        at = lax.rem(y + 4 - k, 4)
        copies.append(pltpu.make_async_copy(refs[k], query.at[at], sems.at[k]))
    for c in copies:
        c.start()
    return copies


def joint_query(query, key_up, chunk):
    pad = jnp.zeros((TOK, 64), bf16)
    low, high = [], []
    for h in range(2):
        latent = dot(query[chunk, :, h * 128 : (h + 1) * 128], key_up[h]).astype(bf16)
        pos = query[chunk, :, 256 + h * 64 : 256 + (h + 1) * 64]
        low.append(jnp.concatenate([latent, pos, pad], axis=1))
        high.append(jnp.concatenate([latent, pad, pos], axis=1))
    return jnp.concatenate(low, axis=0), jnp.concatenate(high, axis=0)


def project(mixed, value_up):
    return [dot(mixed[h * TOK : (h + 1) * TOK], value_up[h]) for h in range(2)]


def new_kernel(q0, q1, q2, q3, key_up, value_up, own, other, stats_out, part_out, query, keys, sems):
    core, xh = coords("core", "xh")
    query_copies = gather_query((q0, q1, q2, q3), query, sems)
    copies = []
    n = 4
    for which, ref in ((core, own), (1 - core, other)):
        for half in range(2):
            for tile in range(2):
                col = pl.ds(pl.multiple_of((which * 2 + tile) * LANES, LANES), LANES)
                copies.append(
                    pltpu.make_async_copy(
                        ref.at[:, :, pl.ds(tile * 64 + half * 32, 32), :],
                        keys.at[:, half, :, :, col],
                        sems.at[n],
                    )
                )
                n += 1
            copies.append(
                pltpu.make_async_copy(
                    ref.at[:, :, pl.ds(128, 16), :],
                    keys.at[:, half, :, pl.ds(pl.multiple_of(which * 16, 16), 16), pl.ds(512, LANES)],
                    sems.at[n],
                )
            )
            n += 1
    for c in copies:
        c.start()
    for c in query_copies:
        c.wait()
    joint = [joint_query(query, key_up, chunk) for chunk in range(4)]
    rows = 2 * TOK
    row_tok = lax.broadcasted_iota(jnp.int32, (rows, TOK), 0) % TOK + xh * TOK
    col = lax.broadcasted_iota(jnp.int32, (rows, TOK), 1)
    col_tok = col // 32 * 64 + col % 32
    causal = [jnp.where(col_tok + 32 * half <= row_tok, 0.0, NEG).astype(f32) for half in range(2)]
    for c in copies:
        c.wait()
    for chunk in range(4):
        scores = []
        for part in range(chunk + 1):
            for half in range(2):
                k = keys[part, half].reshape(TOK, 640)
                s = dot_t(joint[chunk][half], k)
                if part == chunk:
                    s = s + causal[half]
                scores.append(s)
        top = functools.reduce(jnp.maximum, [jnp.max(s, -1, keepdims=True) for s in scores])
        expo = [jnp.exp2((s - top) * EXP_SCALE) for s in scores]
        denom = functools.reduce(jnp.add, [jnp.sum(e, -1, keepdims=True) for e in expo])
        weights = jnp.concatenate([e.astype(bf16) for e in expo], axis=1)
        total = dot(weights, keys[0 : chunk + 1, :, :, :, 0:512].reshape((chunk + 1) * rows, 512))
        stats_out[chunk] = jnp.concatenate(
            [jnp.broadcast_to(top, (rows, 64)), jnp.broadcast_to(denom, (rows, 64))], axis=1
        )
        for h, part in enumerate(project((total / denom).astype(bf16), value_up)):
            part_out[chunk, :, h * 128 : (h + 1) * 128] = part


def cached_kernel(
    cached_len,
    q0,
    q1,
    q2,
    q3,
    key_up,
    value_up,
    own,
    other,
    stats_hbm,
    part_hbm,
    out,
    query,
    keys,
    stats,
    new_part,
    sems,
):
    core, seq = coords("core", "y")
    query_copies = gather_query((q0, q1, q2, q3), query, sems)
    state_copies = [
        pltpu.make_async_copy(stats_hbm, stats, sems.at[20]),
        pltpu.make_async_copy(part_hbm, new_part, sems.at[21]),
    ]
    copies = []
    n = 4
    for which, ref in ((core, own), (1 - core, other)):
        for zp in range(2):
            group = which * 2 + zp
            col = pl.ds(pl.multiple_of(group * LANES, LANES), LANES)
            for half in range(2):
                copies.append(
                    pltpu.make_async_copy(
                        ref.at[:, zp, :, pl.ds(half * PICK_LAT // 2, PICK_LAT // 2), :],
                        keys.at[half, :, :, :, col],
                        sems.at[n],
                    )
                )
                copies.append(
                    pltpu.make_async_copy(
                        ref.at[:, zp, :, pl.ds(PICK_LAT, PICK_PART), :],
                        keys.at[
                            half,
                            :,
                            :,
                            pl.ds(pl.multiple_of(group * PICK_PART, 16), PICK_PART),
                            pl.ds(512, LANES),
                        ],
                        sems.at[n + 1],
                    )
                )
                n += 2
    for c in copies + state_copies:
        c.start()
    for c in query_copies:
        c.wait()
    joint = [joint_query(query, key_up, chunk) for chunk in range(4)]
    count = 4 * PICK_LAT // 2
    index = lax.broadcasted_iota(jnp.int32, (1, count), 1)
    rest = index % (PICK_LAT // 2)
    position = rest // PIECE * 64 + index // (PICK_LAT // 2) * PIECE + rest % PIECE
    length = cached_len[seq]
    bias = [
        jnp.where(position + half * (BLOCKS // 2 * 64) < length, 0.0, NEG).astype(f32)
        for half in range(2)
    ]
    for c in copies + state_copies:
        c.wait()
    for chunk in range(4):
        scores = [
            dot_t(joint[chunk][half], keys[half].reshape(count, 640)) + bias[half]
            for half in range(2)
        ]
        before, denom_before = stats[chunk, :, 0:1], stats[chunk, :, 64:65]
        top = functools.reduce(jnp.maximum, [before] + [jnp.max(s, -1, keepdims=True) for s in scores])
        factor = jnp.exp2((before - top) * EXP_SCALE) * denom_before
        expo = [jnp.exp2((s - top) * EXP_SCALE) for s in scores]
        denom = functools.reduce(jnp.add, [factor] + [jnp.sum(e, -1, keepdims=True) for e in expo])
        weights = jnp.concatenate([e.astype(bf16) for e in expo], axis=1)
        total = dot(weights, keys[:, :, :, :, 0:512].reshape(2 * count, 512))
        share = factor / denom
        for h, part in enumerate(project((total / denom).astype(bf16), value_up)):
            tok = slice(h * TOK, (h + 1) * TOK)
            cols = slice(h * 128, (h + 1) * 128)
            out[chunk, :, cols] = (part + new_part[chunk, :, cols] * share[tok]).astype(bf16)


def smem():
    return pl.BlockSpec(memory_space=pltpu.SMEM)


def vmem():
    return pl.BlockSpec(memory_space=pltpu.VMEM)


def anywhere():
    return pl.BlockSpec(memory_space=pl.ANY)


def params(mib):
    return pltpu.CompilerParams(vmem_limit_bytes=mib * MIB)


def shape(dims, kind=bf16):
    return jax.ShapeDtypeStruct(dims, kind)


def on_device(
    query_nope,
    query_rope,
    key_up,
    value_up,
    new_latent,
    new_rope,
    cache_latent,
    cache_rope,
    block_owner,
    block_slot,
    cached_len,
):
    y = lax.axis_index("y")
    send = pl.pallas_call(
        pack_kernel,
        out_shape=shape((SEQS, 4, MSG_ROWS, LANES)),
        in_specs=[anywhere()] * 6,
        out_specs=anywhere(),
        scratch_shapes=[
            pltpu.SMEM((SEQS, BLOCKS), jnp.int32),
            pltpu.SMEM((SEQS, BLOCKS), jnp.int32),
            pltpu.SMEM((16,), jnp.int32),
            pltpu.VMEM((CAP, 64, LANES), bf16),
            pltpu.VMEM((CAP, 64, 64), bf16),
            pltpu.VMEM((SEQS, 64, 2 * LANES), bf16),
            pltpu.VMEM((SEQS, 64, TOK), bf16),
            pltpu.VMEM((SEQS, TOK, 64), bf16),
            pltpu.VMEM((4, NEW_AT, LANES), bf16),
            pltpu.VMEM((SEQS, NEW_ROWS, LANES), bf16),
            pltpu.SemaphoreType.DMA((4 + 2 * CAP,)),
            pltpu.SemaphoreType.DMA((8,)),
        ],
        compiler_params=params(63),
        name="pack",
    )(block_owner, block_slot, cache_latent, cache_rope, new_latent, jnp.swapaxes(new_rope, 1, 2))
    send, query_nope, query_rope, owner = lax.optimization_barrier(
        (send, query_nope, query_rope, block_owner)
    )
    recv = lax.all_to_all(send.reshape(16, MSG_ROWS, LANES), PLANE, 0, 0)
    query = jnp.concatenate([query_nope, query_rope], -1)
    queries = []
    for k in range(4):
        part = lax.dynamic_index_in_dim(query, lax.rem(y + k, 4), 0, keepdims=False)
        if k:
            part = lax.ppermute(part, "y", [(i, (i + k) % 4) for i in range(4)])
        queries.append(part)
    plan = pl.pallas_call(
        plan_kernel,
        out_shape=shape((2, BLOCKS), jnp.int32),
        in_specs=[smem()],
        out_specs=smem(),
        scratch_shapes=[pltpu.SMEM((16,), jnp.int32)],
        name="plan",
    )(owner)
    recv, plan = lax.optimization_barrier((recv, plan))

    picked, new_own = pl.pallas_call(
        select_kernel,
        out_shape=(shape((8, PICK_ROWS, LANES)), shape((16, NEW_ROWS, LANES))),
        in_specs=[smem(), anywhere()],
        out_specs=(vmem(), vmem()),
        scratch_shapes=[
            pltpu.VMEM((PICK_LAT, LANES), bf16),
            pltpu.VMEM((BLOCKS, PIECE, LANES), bf16),
            pltpu.VMEM((BLOCKS // 2 * PIECE, LANES), bf16),
            pltpu.VMEM((16, NEW_ROWS, LANES), bf16),
            pltpu.SemaphoreType.DMA((2 * BLOCKS + 1,)),
        ],
        compiler_params=params(16),
        name="select",
    )(plan, recv)
    picked, new_own, *queries = lax.optimization_barrier((picked, new_own, *queries))
    swap = [(0, 1), (1, 0)]
    new_own = new_own.reshape(4, 4, NEW_ROWS, LANES)
    new_other = lax.ppermute(new_own, "core", swap)
    cache_own = lax.all_to_all(picked, SPREAD, 0, 0).reshape(2, 2, 2, PICK_ROWS, LANES)

    rows = 2 * TOK
    stats, part = pl.pallas_call(
        new_kernel,
        out_shape=(shape((4, rows, LANES), f32), shape((4, TOK, 256), f32)),
        in_specs=[anywhere()] * 4 + [vmem()] * 2 + [anywhere()] * 2,
        out_specs=(vmem(), vmem()),
        scratch_shapes=[
            pltpu.VMEM((4, TOK, 384), bf16),
            pltpu.VMEM((4, 2, 4, 32, 640), bf16),
            pltpu.SemaphoreType.DMA((16,)),
        ],
        compiler_params=params(32),
        cost_estimate=pl.CostEstimate(flops=3 * 10**9, bytes_accessed=5 * 10**6, transcendentals=700000),
        name="attend_new",
    )(*queries, key_up, value_up, new_own, new_other)
    cache_own, stats, part = lax.optimization_barrier((cache_own, stats, part))
    cache_other = lax.ppermute(cache_own, "core", swap)
    mixed = pl.pallas_call(
        cached_kernel,
        out_shape=shape((4, TOK, 256)),
        in_specs=[smem()] + [anywhere()] * 4 + [vmem()] * 2 + [anywhere()] * 4,
        out_specs=vmem(),
        scratch_shapes=[
            pltpu.VMEM((4, TOK, 384), bf16),
            pltpu.VMEM((2, 2, 2, PICK_LAT // 2, 640), bf16),
            pltpu.VMEM((4, rows, LANES), f32),
            pltpu.VMEM((4, TOK, 256), f32),
            pltpu.SemaphoreType.DMA((22,)),
        ],
        compiler_params=params(32),
        cost_estimate=pl.CostEstimate(flops=4 * 10**9, bytes_accessed=5 * 10**6, transcendentals=1600000),
        name="attend_cached",
    )(cached_len, *queries, key_up, value_up, cache_own, cache_other, stats, part)
    return lax.all_to_all(mixed, "y", 0, 0)


def solution(mesh):
    fine = Mesh(
        mesh.devices.reshape(4, 2, 8, 2, 2, 2), ("y", "xh", "zh", "zp", "core", "xl")
    )
    ctx = ("y", "xh")
    heads = ("zh", "zp", "core", "xl")
    holders = ("y", "xh", "xl")
    return jax.shard_map(
        on_device,
        mesh=fine,
        in_specs=(
            P(None, ctx, heads),
            P(None, ctx, heads),
            P(heads, None, None),
            P(heads, None, None),
            P(None, ctx, None),
            P(None, ctx, None),
            P(holders, None, None),
            P(holders, None, None),
            P(),
            P(),
            P(),
        ),
        out_specs=P(None, ctx, heads),
        check_vma=False,
    )
```

```python
import functools

import jax
import jax.numpy as jnp
from jax import lax
from jax.experimental import pallas as pl
from jax.experimental.pallas import tpu as pltpu
from jax.sharding import Mesh
from jax.sharding import PartitionSpec as P

NEG = -1e30
LOG2E = 1.4426950408889634
EXP_SCALE = 192.0 ** (-0.5) * LOG2E
HOLDER = ("y", "xh", "xl")
PLANE = ("xl", "xh", "y")
SPREAD = ("xl", "xh", "zp")
CAP = 9
PIECE = 16
LANES = 128
SEQS = 4
BLOCKS = 24
TOK = 128
LAT_ROWS = CAP * PIECE
ROPE_ROWS = (CAP + 1) // 2 * PIECE
NEW_AT = LAT_ROWS + ROPE_ROWS
NEW_ROWS = 2 * 64 + 16
MSG_ROWS = NEW_AT + NEW_ROWS
PICK_LAT = BLOCKS * PIECE
PICK_PART = BLOCKS // 2 * PIECE // 4
PICK_ROWS = PICK_LAT + PICK_PART
MIB = 1024 * 1024
bf16 = jnp.bfloat16
f32 = jnp.float32


def coords(*names):
    return [lax.axis_index(n) for n in names]


def pack_kernel(
    owner,
    slot,
    cache_latent,
    cache_rope,
    new_latent,
    new_rope,
    out,
    owners,
    places,
    slots,
    lat,
    rope,
    nlat,
    nrope_t,
    nrope,
    cached_part,
    new_part,
    sems,
    out_sems,
):
    holder, core, xl, zp = coords(HOLDER, "core", "xl", "zp")
    table_copies = [
        pltpu.make_async_copy(owner, owners, sems.at[4]),
        pltpu.make_async_copy(slot, places, sems.at[5]),
    ]
    for c in table_copies:
        c.start()
    cols = pl.ds(pl.multiple_of((core * 2 + zp) * LANES, LANES), LANES)
    half = pl.ds(pl.multiple_of(core * 2 * LANES, 2 * LANES), 2 * LANES)
    rows = pl.ds(pl.multiple_of(xl * 64, 64), 64)
    new_copies = [
        pltpu.make_async_copy(new_latent.at[:, rows, half], nlat, sems.at[0]),
        pltpu.make_async_copy(new_rope, nrope_t, sems.at[1]),
    ]
    pool_copies = [
        pltpu.make_async_copy(cache_latent.at[:, :, cols], lat, sems.at[2]),
        pltpu.make_async_copy(cache_rope, rope, sems.at[3]),
    ]
    for c in new_copies + pool_copies:
        c.start()
    for r in range(CAP):
        slots[r] = 0
    for c in table_copies:
        c.wait()
    count = jnp.int32(0)
    for s in range(SEQS):
        for j in range(BLOCKS):
            hit = owners[s, j] == holder
            slots[jnp.where(hit, jnp.minimum(count, CAP), CAP)] = places[s, j]
            count = count + hit.astype(jnp.int32)
    for c in new_copies:
        c.wait()
    low = pl.ds(pl.multiple_of(xl * 64 + core * 16, 16), 16)
    high = pl.ds(pl.multiple_of(xl * 64 + 32 + core * 16, 16), 16)
    for s in range(SEQS):
        nrope[s] = nrope_t[s].T
        new_part[s, 0:64, :] = nlat[s, :, 0:LANES]
        new_part[s, 64:128, :] = nlat[s, :, LANES : 2 * LANES]
        new_part[s, 128:144, :] = jnp.concatenate([nrope[s, low, :], nrope[s, high, :]], axis=1)
    out_copies = [
        pltpu.make_async_copy(new_part, out.at[x, :, pl.ds(NEW_AT, NEW_ROWS), :], out_sems.at[x])
        for x in range(4)
    ]
    for c in out_copies:
        c.start()
    flipped = (0, 2, 1, 3)
    for c in pool_copies:
        c.wait()
    blocks = [slots[r] for r in range(CAP)]
    for r in range(CAP):
        for i, x in enumerate(flipped):
            cached_part[i, r * PIECE : (r + 1) * PIECE, :] = lat[blocks[r], x * PIECE : (x + 1) * PIECE, :]
    for m in range((CAP + 1) // 2):
        first = rope[blocks[2 * m]]
        second = rope[blocks[2 * m + 1]] if 2 * m + 1 < CAP else first
        both = jnp.concatenate([first, second], axis=1)
        for i, x in enumerate(flipped):
            cached_part[i, LAT_ROWS + m * PIECE : LAT_ROWS + (m + 1) * PIECE, :] = both[
                x * PIECE : (x + 1) * PIECE, :
            ]
    for s in range(SEQS):
        c = pltpu.make_async_copy(cached_part, out.at[:, s, pl.ds(0, NEW_AT), :], out_sems.at[4 + s])
        c.start()
        out_copies.append(c)
    for c in out_copies:
        c.wait()


def plan_kernel(owner, plan, counts):
    for h in range(16):
        counts[h] = 0
    for s in range(SEQS):
        for j in range(BLOCKS):
            h = owner[s, j]
            rank = counts[h]
            counts[h] = rank + 1
            source = (h % 2 * 2 + h // 2 % 2) * 4 + h // 4
            plan[s, j] = source * 16 + jnp.minimum(rank, CAP - 1)


def select_kernel(plan, recv, out, new_out, picked, tiles, pairs, sems, out_sems):
    core, zp, seq = coords("core", "zp", "y")
    entries = [plan[seq, j] for j in range(BLOCKS)]
    ranks = [e % 16 for e in entries]
    sources = [e // 16 for e in entries]
    rope_copies, lat_copies = [], []
    for j in range(BLOCKS):
        c = pltpu.make_async_copy(
            recv.at[sources[j], pl.ds(pl.multiple_of(LAT_ROWS + ranks[j] // 2 * PIECE, PIECE), PIECE), :],
            tiles.at[j],
            sems.at[2 * j + 1],
        )
        c.start()
        rope_copies.append(c)
    for j in range(BLOCKS):
        c = pltpu.make_async_copy(
            recv.at[sources[j], pl.ds(pl.multiple_of(ranks[j] * PIECE, PIECE), PIECE), :],
            picked.at[pl.ds(j * PIECE, PIECE), :],
            sems.at[2 * j],
        )
        c.start()
        lat_copies.append(c)
    new_copy = pltpu.make_async_copy(
        recv.at[:, pl.ds(NEW_AT, NEW_ROWS), :], new_out, sems.at[2 * BLOCKS]
    )
    new_copy.start()
    for c in rope_copies:
        c.wait()
    for j in range(BLOCKS // 2):
        k = j + BLOCKS // 2
        first = jnp.where(ranks[j] % 2 == 1, tiles[j, :, 64:128], tiles[j, :, 0:64])
        second = jnp.where(ranks[k] % 2 == 1, tiles[k, :, 64:128], tiles[k, :, 0:64])
        pairs[j * PIECE : (j + 1) * PIECE, :] = jnp.concatenate([first, second], axis=1)
    part = pl.ds(pl.multiple_of((core * 2 + zp) * PICK_PART, 16), PICK_PART)
    picked[PICK_LAT:PICK_ROWS, :] = pairs[part, :]
    for c in lat_copies:
        c.wait()
    out_copies = [pltpu.make_async_copy(picked, out.at[d], out_sems.at[d]) for d in range(8)]
    for c in out_copies:
        c.start()
    for c in out_copies + [new_copy]:
        c.wait()


def dot(a, b):
    return lax.dot_general(a, b, (((1,), (0,)), ((), ())), preferred_element_type=f32)


def dot_t(a, b):
    return lax.dot_general(a, b, (((1,), (1,)), ((), ())), preferred_element_type=f32)


def gather_query(refs, query, sems):
    (y,) = coords("y")
    copies = []
    for k in range(4):
        at = lax.rem(y + 4 - k, 4)
        copies.append(pltpu.make_async_copy(refs[k], query.at[at], sems.at[k]))
    for c in copies:
        c.start()
    return copies


def halves(core):
    return [pl.ds(pl.multiple_of(c * 256, 256), 256) for c in (core, 1 - core)]


def joint_query(query, key_up, core, chunk, joint):
    pad = jnp.zeros((TOK, 64), bf16)
    for h in range(2):
        rows = pl.ds((2 * chunk + h) * TOK, TOK)
        nope = query[chunk, :, h * 128 : (h + 1) * 128]
        pos = query[chunk, :, 256 + h * 64 : 256 + (h + 1) * 64]
        for i, cols in enumerate(halves(core)):
            joint[rows, i * 256 : (i + 1) * 256] = dot(nope, key_up[h, :, cols]).astype(bf16)
        joint[rows, 512:640] = jnp.concatenate([pos, pad], axis=1)
        joint[rows, 640:768] = jnp.concatenate([pad, pos], axis=1)


def load_query(joint, start, count):
    low = joint[start : start + count, 0:640]
    high = jnp.concatenate([joint[start : start + count, 0:512], joint[start : start + count, 640:768]], axis=1)
    return low, high


def project(mixed, value_up, core, h):
    own, other = halves(core)
    return dot(mixed[:, 0:256], value_up[h, own, :]) + dot(mixed[:, 256:512], value_up[h, other, :])


def new_kernel(
    q0, q1, q2, q3, key_up, value_up, own, other, stats_out, part_out, token, query, joint, keys, sems
):
    core, xh = coords("core", "xh")
    query_copies = gather_query((q0, q1, q2, q3), query, sems)
    token[...] = jnp.zeros_like(token)
    for i, (which, ref) in enumerate(((core, own), (1 - core, other))):
        rope_rows = pl.ds(pl.multiple_of(which * 16, 16), 16)
        for y in range(4):
            for part in range(4):
                for half in range(2):
                    for tile in range(2):
                        at = tile * 64 + half * 32
                        col = (2 * i + tile) * LANES
                        keys[y, half, part, :, col : col + LANES] = ref[part % 2, part // 2, y, at : at + 32, :]
                    keys[y, half, part, rope_rows, 512:640] = ref[part % 2, part // 2, y, 128:144, :]
    for c in query_copies:
        c.wait()
    for chunk in range(4):
        joint_query(query, key_up, core, chunk, joint)
    rows = 2 * TOK
    row_tok = lax.broadcasted_iota(jnp.int32, (rows, TOK), 0) % TOK + xh * TOK
    col = lax.broadcasted_iota(jnp.int32, (rows, TOK), 1)
    col_tok = col // 32 * 64 + col % 32
    lane = lax.broadcasted_iota(jnp.int32, (rows, LANES), 1)
    causal = [jnp.where(col_tok + 32 * half <= row_tok, 0.0, NEG).astype(f32) for half in range(2)]
    for chunk in range(4):
        q = load_query(joint, chunk * rows, rows)
        scores = []
        for part in range(chunk + 1):
            for half in range(2):
                s = dot_t(q[half], keys[part, half].reshape(TOK, 640))
                if part == chunk:
                    s = s + causal[half]
                scores.append(s)
        top = functools.reduce(jnp.maximum, [jnp.max(s, -1, keepdims=True) for s in scores])
        expo = [jnp.exp2((s - top) * EXP_SCALE) for s in scores]
        denom = functools.reduce(jnp.add, [jnp.sum(e, -1, keepdims=True) for e in expo])
        weights = jnp.concatenate([e.astype(bf16) for e in expo], axis=1)
        total = dot(weights, keys[0 : chunk + 1, :, :, :, 0:512].reshape((chunk + 1) * rows, 512))
        stats_out[:, chunk * rows : (chunk + 1) * rows] = jnp.where(lane == 0, top, denom).T[0:8]
        mixed = (total / denom).astype(bf16)
        for h in range(2):
            part_out[chunk, :, h * 128 : (h + 1) * 128] = project(
                mixed[h * TOK : (h + 1) * TOK], value_up, core, h
            )


def cached_kernel(
    cached_len,
    q0,
    q1,
    q2,
    q3,
    key_up,
    value_up,
    own,
    other,
    stats,
    new_part,
    token,
    out,
    query,
    joint,
    keys,
    sems,
):
    core, seq = coords("core", "y")
    query_copies = gather_query((q0, q1, q2, q3), query, sems)
    span = PICK_LAT // 2
    for i, (which, ref) in enumerate(((core, own), (1 - core, other))):
        for zp in range(2):
            rope_at = (which * 2 + zp) * PICK_PART
            for x in range(4):
                for half in range(2):
                    keys[half, x * span : (x + 1) * span, (2 * i + zp) * LANES : (2 * i + zp + 1) * LANES] = ref[
                        x % 2, x // 2, zp, half * span : (half + 1) * span, :
                    ]
                    keys[half, pl.ds(pl.multiple_of(x * span + rope_at, 16), PICK_PART), 512:640] = ref[
                        x % 2, x // 2, zp, PICK_LAT:PICK_ROWS, :
                    ]
    count = 4 * span
    index = lax.broadcasted_iota(jnp.int32, (1, count), 1)
    rest = index % span
    position = rest // PIECE * 64 + index // span * PIECE + rest % PIECE
    length = cached_len[seq]
    bias = [
        jnp.where(position + half * (BLOCKS // 2 * 64) < length, 0.0, NEG).astype(f32)
        for half in range(2)
    ]
    for c in query_copies:
        c.wait()
    for chunk in range(4):
        joint_query(query, key_up, core, chunk, joint)
    rows = 4 * TOK
    for group in range(2):
        at = slice(group * rows, (group + 1) * rows)
        q = load_query(joint, group * rows, rows)
        scores = [dot_t(q[half], keys[half]) + bias[half] for half in range(2)]
        state = jnp.concatenate([stats[:, at]] * 16, axis=0).T
        before, denom_before = state[:, 0:1], state[:, 1:2]
        top = functools.reduce(jnp.maximum, [before] + [jnp.max(s, -1, keepdims=True) for s in scores])
        factor = jnp.exp2((before - top) * EXP_SCALE) * denom_before
        expo = [jnp.exp2((s - top) * EXP_SCALE) for s in scores]
        denom = functools.reduce(jnp.add, [factor] + [jnp.sum(e, -1, keepdims=True) for e in expo])
        weights = jnp.concatenate([e.astype(bf16) for e in expo], axis=1)
        total = dot(weights, keys[:, :, 0:512].reshape(2 * count, 512))
        share = factor / denom
        mixed = (total / denom).astype(bf16)
        for c in range(2):
            chunk = group * 2 + c
            for h in range(2):
                tok = slice((2 * c + h) * TOK, (2 * c + h + 1) * TOK)
                cols = slice(h * 128, (h + 1) * 128)
                fresh = project(mixed[tok], value_up, core, h)
                out[chunk, :, cols] = (fresh + new_part[chunk, :, cols] * share[tok]).astype(bf16)


def smem():
    return pl.BlockSpec(memory_space=pltpu.SMEM)


def vmem():
    return pl.BlockSpec(memory_space=pltpu.VMEM)


def anywhere():
    return pl.BlockSpec(memory_space=pl.ANY)


def params(mib):
    return pltpu.CompilerParams(vmem_limit_bytes=mib * MIB)


def shape(dims, kind=bf16):
    return jax.ShapeDtypeStruct(dims, kind)


def on_device(
    query_nope,
    query_rope,
    key_up,
    value_up,
    new_latent,
    new_rope,
    cache_latent,
    cache_rope,
    block_owner,
    block_slot,
    cached_len,
):
    y = lax.axis_index("y")
    send = pl.pallas_call(
        pack_kernel,
        out_shape=shape((4, SEQS, MSG_ROWS, LANES)),
        in_specs=[anywhere()] * 6,
        out_specs=anywhere(),
        scratch_shapes=[
            pltpu.SMEM((SEQS, BLOCKS), jnp.int32),
            pltpu.SMEM((SEQS, BLOCKS), jnp.int32),
            pltpu.SMEM((16,), jnp.int32),
            pltpu.VMEM((32, 64, LANES), bf16),
            pltpu.VMEM((32, 64, 64), bf16),
            pltpu.VMEM((SEQS, 64, 2 * LANES), bf16),
            pltpu.VMEM((SEQS, 64, TOK), bf16),
            pltpu.VMEM((SEQS, TOK, 64), bf16),
            pltpu.VMEM((4, NEW_AT, LANES), bf16),
            pltpu.VMEM((SEQS, NEW_ROWS, LANES), bf16),
            pltpu.SemaphoreType.DMA((6,)),
            pltpu.SemaphoreType.DMA((8,)),
        ],
        compiler_params=params(63),
        name="pack",
    )(block_owner, block_slot, cache_latent, cache_rope, new_latent, jnp.swapaxes(new_rope, 1, 2))
    send, query_nope, query_rope, owner = lax.optimization_barrier(
        (send, query_nope, query_rope, block_owner)
    )
    plan = pl.pallas_call(
        plan_kernel,
        out_shape=shape((SEQS, BLOCKS), jnp.int32),
        in_specs=[smem()],
        out_specs=smem(),
        scratch_shapes=[pltpu.SMEM((16,), jnp.int32)],
        name="plan",
    )(owner)
    recv = lax.all_to_all(send.reshape(16, MSG_ROWS, LANES), PLANE, 0, 0)
    query = jnp.concatenate([query_nope, query_rope], -1)
    queries = []
    for k in range(4):
        part = lax.dynamic_index_in_dim(query, lax.rem(y + k, 4), 0, keepdims=False)
        if k == 3:
            part, plan = lax.optimization_barrier((part, plan))
        if k:
            part = lax.ppermute(part, "y", [(i, (i + k) % 4) for i in range(4)])
        queries.append(part)
    picked, new_own = pl.pallas_call(
        select_kernel,
        out_shape=(shape((8, PICK_ROWS, LANES)), shape((16, NEW_ROWS, LANES))),
        in_specs=[smem(), anywhere()],
        out_specs=(anywhere(), anywhere()),
        scratch_shapes=[
            pltpu.VMEM((PICK_ROWS, LANES), bf16),
            pltpu.VMEM((BLOCKS, PIECE, LANES), bf16),
            pltpu.VMEM((BLOCKS // 2 * PIECE, LANES), bf16),
            pltpu.SemaphoreType.DMA((2 * BLOCKS + 1,)),
            pltpu.SemaphoreType.DMA((8,)),
        ],
        compiler_params=params(16),
        name="select",
    )(plan, recv)
    picked, new_own, *queries = lax.optimization_barrier((picked, new_own, *queries))
    swap = [(0, 1), (1, 0)]
    new_own = new_own.reshape(2, 2, 4, NEW_ROWS, LANES)
    new_other = lax.ppermute(new_own, "core", swap)
    cache_own = lax.all_to_all(picked, SPREAD, 0, 0).reshape(2, 2, 2, PICK_ROWS, LANES)

    rows = 8 * TOK
    stats, part, token = pl.pallas_call(
        new_kernel,
        out_shape=(
            shape((8, rows), f32),
            shape((4, TOK, 256), f32),
            shape((8, LANES), f32),
        ),
        in_specs=[anywhere()] * 4 + [vmem()] * 4,
        out_specs=(vmem(),) * 3,
        scratch_shapes=[
            pltpu.VMEM((4, TOK, 384), bf16),
            pltpu.VMEM((rows, 768), bf16),
            pltpu.VMEM((4, 2, 4, 32, 640), bf16),
            pltpu.SemaphoreType.DMA((4,)),
        ],
        compiler_params=params(24),
        cost_estimate=pl.CostEstimate(flops=3 * 10**9, bytes_accessed=5 * 10**6, transcendentals=700000),
        name="attend_new",
    )(*queries, key_up, value_up, new_own, new_other)
    cache_own, token = lax.optimization_barrier((cache_own, token))
    cache_other = lax.ppermute(cache_own, "core", swap)
    mixed = pl.pallas_call(
        cached_kernel,
        out_shape=shape((4, TOK, 256)),
        in_specs=[smem()] + [anywhere()] * 4 + [vmem()] * 7,
        out_specs=vmem(),
        scratch_shapes=[
            pltpu.VMEM((4, TOK, 384), bf16),
            pltpu.VMEM((rows, 768), bf16),
            pltpu.VMEM((2, 4 * PICK_LAT // 2, 640), bf16),
            pltpu.SemaphoreType.DMA((4,)),
        ],
        compiler_params=params(24),
        cost_estimate=pl.CostEstimate(flops=4 * 10**9, bytes_accessed=5 * 10**6, transcendentals=1600000),
        name="attend_cached",
    )(cached_len, *queries, key_up, value_up, cache_own, cache_other, stats, part, token)
    return lax.all_to_all(mixed, "y", 0, 0)


def solution(mesh):
    fine = Mesh(
        mesh.devices.reshape(4, 2, 8, 2, 2, 2), ("y", "xh", "zh", "zp", "core", "xl")
    )
    ctx = ("y", "xh")
    heads = ("zh", "zp", "core", "xl")
    holders = ("y", "xh", "xl")
    return jax.shard_map(
        on_device,
        mesh=fine,
        in_specs=(
            P(None, ctx, heads),
            P(None, ctx, heads),
            P(heads, None, None),
            P(heads, None, None),
            P(None, ctx, None),
            P(None, ctx, None),
            P(holders, None, None),
            P(holders, None, None),
            P(),
            P(),
            P(),
        ),
        out_specs=P(None, ctx, heads),
        check_vma=False,
    )
```

```python
import functools

import jax
import jax.numpy as jnp
from jax import lax
from jax.experimental import pallas as pl
from jax.experimental.pallas import tpu as pltpu
from jax.sharding import Mesh
from jax.sharding import PartitionSpec as P

NEG = -1e30
LOG2E = 1.4426950408889634
EXP_SCALE = 192.0 ** (-0.5) * LOG2E
HOLDER = ("y", "xh", "xl")
PLANE = ("xl", "xh", "y")
SPREAD = ("xl", "xh", "zp")
CAP = 9
PIECE = 16
LANES = 128
SEQS = 4
BLOCKS = 24
TOK = 128
LAT_ROWS = CAP * PIECE
ROPE_ROWS = (CAP + 3) // 4 * PIECE
NEW_AT = LAT_ROWS + ROPE_ROWS
NEW_ROWS = 2 * 64 + 16
MSG_ROWS = NEW_AT + NEW_ROWS
PICK_LAT = BLOCKS * PIECE
PICK_PART = BLOCKS // 4 * PIECE // 2
PICK_ROWS = PICK_LAT + PICK_PART
MIB = 1024 * 1024
bf16 = jnp.bfloat16
f32 = jnp.float32


def coords(*names):
    return [lax.axis_index(n) for n in names]


def pack_kernel(
    owner,
    slot,
    cache_latent,
    cache_rope,
    new_latent,
    new_rope,
    out,
    owners,
    places,
    slots,
    lat,
    rope,
    nlat,
    nrope_t,
    nrope,
    cached_part,
    new_part,
    sems,
    out_sems,
):
    holder, core, xl, zp = coords(HOLDER, "core", "xl", "zp")
    table_copies = [
        pltpu.make_async_copy(owner, owners, sems.at[4]),
        pltpu.make_async_copy(slot, places, sems.at[5]),
    ]
    for c in table_copies:
        c.start()
    cols = pl.ds(pl.multiple_of((core * 2 + zp) * LANES, LANES), LANES)
    half = pl.ds(pl.multiple_of(core * 2 * LANES, 2 * LANES), 2 * LANES)
    rows = pl.ds(pl.multiple_of(xl * 64, 64), 64)
    new_copies = [
        pltpu.make_async_copy(new_latent.at[:, rows, half], nlat, sems.at[0]),
        pltpu.make_async_copy(new_rope, nrope_t, sems.at[1]),
    ]
    pool_copies = [
        pltpu.make_async_copy(cache_latent.at[:, :, cols], lat, sems.at[2]),
        pltpu.make_async_copy(cache_rope, rope, sems.at[3]),
    ]
    for c in new_copies + pool_copies:
        c.start()
    for r in range(CAP):
        slots[r] = 0
    for c in table_copies:
        c.wait()
    count = jnp.int32(0)
    for s in range(SEQS):
        for j in range(BLOCKS):
            hit = owners[s, j] == holder
            slots[jnp.where(hit, jnp.minimum(count, CAP), CAP)] = places[s, j]
            count = count + hit.astype(jnp.int32)
    for c in new_copies:
        c.wait()
    low = pl.ds(pl.multiple_of(xl * 64 + core * 16, 16), 16)
    high = pl.ds(pl.multiple_of(xl * 64 + 32 + core * 16, 16), 16)
    for s in range(SEQS):
        nrope[s] = nrope_t[s].T
        new_part[s, 0:64, :] = nlat[s, :, 0:LANES]
        new_part[s, 64:128, :] = nlat[s, :, LANES : 2 * LANES]
        new_part[s, 128:144, :] = jnp.concatenate([nrope[s, low, :], nrope[s, high, :]], axis=1)
    out_copies = [
        pltpu.make_async_copy(new_part, out.at[x, :, pl.ds(NEW_AT, NEW_ROWS), :], out_sems.at[x])
        for x in range(4)
    ]
    for c in out_copies:
        c.start()
    flipped = (0, 2, 1, 3)
    for c in pool_copies:
        c.wait()
    blocks = [slots[r] for r in range(CAP)]
    for r in range(CAP):
        for i, x in enumerate(flipped):
            cached_part[i, r * PIECE : (r + 1) * PIECE, :] = lat[blocks[r], x * PIECE : (x + 1) * PIECE, :]
    for m in range((CAP + 3) // 4):
        quarter = []
        for r in range(4 * m, 4 * m + 4):
            whole = rope[blocks[min(r, CAP - 1)]]
            quarter.append(jnp.where(core == 0, whole[:, 0:32], whole[:, 32:64]))
        both = jnp.concatenate(quarter, axis=1)
        for i, x in enumerate(flipped):
            cached_part[i, LAT_ROWS + m * PIECE : LAT_ROWS + (m + 1) * PIECE, :] = both[
                x * PIECE : (x + 1) * PIECE, :
            ]
    for s in range(SEQS):
        c = pltpu.make_async_copy(cached_part, out.at[:, s, pl.ds(0, NEW_AT), :], out_sems.at[4 + s])
        c.start()
        out_copies.append(c)
    for c in out_copies:
        c.wait()


def plan_kernel(owner, plan):
    low, high = jnp.int32(0), jnp.int32(0)
    for s in range(SEQS):
        for j in range(BLOCKS):
            h = owner[s, j]
            shift = (h & 7) * 4
            first = h < 8
            rank = (jnp.where(first, low, high) >> shift) & 15
            one = jnp.int32(1) << shift
            low = low + jnp.where(first, one, 0)
            high = high + jnp.where(first, 0, one)
            source = ((h & 1) * 2 + ((h >> 1) & 1)) * 4 + (h >> 2)
            plan[s, j] = source * 16 + jnp.minimum(rank, CAP - 1)


def select_kernel(plan, recv, out, new_out, cached, picked, packed, sems, out_sems):
    zp, seq = coords("zp", "y")
    arrive = pltpu.make_async_copy(recv.at[:, pl.ds(0, NEW_AT), :], cached, sems.at[0])
    arrive.start()
    entries = [plan[seq, j] for j in range(BLOCKS)]
    ranks = [e & 15 for e in entries]
    sources = [e >> 4 for e in entries]
    new_copy = pltpu.make_async_copy(
        recv.at[:, pl.ds(NEW_AT, NEW_ROWS), :], new_out, sems.at[1]
    )
    new_copy.start()
    arrive.wait()
    for j in range(BLOCKS):
        rows = pl.ds(pl.multiple_of(ranks[j] * PIECE, PIECE), PIECE)
        picked[j * PIECE : (j + 1) * PIECE, :] = cached[sources[j], rows, :]

    def rotary(j):
        rows = pl.ds(pl.multiple_of(LAT_ROWS + (ranks[j] >> 2) * PIECE, PIECE), PIECE)
        tile = cached[sources[j], rows, :]
        odd = (ranks[j] & 1) == 1
        left = jnp.where(odd, tile[:, 32:64], tile[:, 0:32])
        right = jnp.where(odd, tile[:, 96:128], tile[:, 64:96])
        return jnp.where((ranks[j] & 2) == 2, right, left)

    for j in range(BLOCKS // 4):
        packed[j * PIECE : (j + 1) * PIECE, :] = jnp.concatenate(
            [rotary(j + e * BLOCKS // 4) for e in range(4)], axis=1
        )
    picked[PICK_LAT:PICK_ROWS, :] = packed[pl.ds(pl.multiple_of(zp * PICK_PART, 16), PICK_PART), :]
    out_copies = [pltpu.make_async_copy(picked, out.at[d], out_sems.at[d]) for d in range(8)]
    for c in out_copies:
        c.start()
    for c in out_copies + [new_copy]:
        c.wait()


def dot(a, b):
    return lax.dot_general(a, b, (((1,), (0,)), ((), ())), preferred_element_type=f32)


def dot_t(a, b):
    return lax.dot_general(a, b, (((1,), (1,)), ((), ())), preferred_element_type=f32)


def gather_query(refs, query, sems):
    (y,) = coords("y")
    copies = []
    for k in range(4):
        at = lax.rem(y + 4 - k, 4)
        copies.append(pltpu.make_async_copy(refs[k], query.at[at], sems.at[k]))
    for c in copies:
        c.start()
    return copies


def halves(core):
    return [pl.ds(pl.multiple_of(c * 256, 256), 256) for c in (core, 1 - core)]


def joint_query(query, key_up, core, chunk, joint):
    pad = jnp.zeros((TOK, 64), bf16)
    for h in range(2):
        rows = pl.ds((2 * chunk + h) * TOK, TOK)
        nope = query[chunk, :, h * 128 : (h + 1) * 128]
        pos = query[chunk, :, 256 + h * 64 : 256 + (h + 1) * 64]
        for i, cols in enumerate(halves(core)):
            joint[rows, i * 256 : (i + 1) * 256] = dot(nope, key_up[h, :, cols]).astype(bf16)
        joint[rows, 512:640] = jnp.concatenate([pos, pad], axis=1)
        joint[rows, 640:768] = jnp.concatenate([pad, pos], axis=1)


def load_query(joint, start, count):
    low = joint[start : start + count, 0:640]
    high = jnp.concatenate([joint[start : start + count, 0:512], joint[start : start + count, 640:768]], axis=1)
    return low, high


def project(mixed, value_up, core, h):
    own, other = halves(core)
    return dot(mixed[:, 0:256], value_up[h, own, :]) + dot(mixed[:, 256:512], value_up[h, other, :])


def new_kernel(
    q0, q1, q2, q3, key_up, value_up, own, other, stats_out, part_out, token, query, joint, keys, sems
):
    core, xh = coords("core", "xh")
    query_copies = gather_query((q0, q1, q2, q3), query, sems)
    token[...] = jnp.zeros_like(token)
    for i, (which, ref) in enumerate(((core, own), (1 - core, other))):
        rope_rows = pl.ds(pl.multiple_of(which * 16, 16), 16)
        for y in range(4):
            for part in range(4):
                for half in range(2):
                    for tile in range(2):
                        at = tile * 64 + half * 32
                        col = (2 * i + tile) * LANES
                        keys[y, half, part, :, col : col + LANES] = ref[part % 2, part // 2, y, at : at + 32, :]
                    keys[y, half, part, rope_rows, 512:640] = ref[part % 2, part // 2, y, 128:144, :]
    for c in query_copies:
        c.wait()
    for chunk in range(4):
        joint_query(query, key_up, core, chunk, joint)
    rows = 2 * TOK
    row_tok = lax.broadcasted_iota(jnp.int32, (rows, TOK), 0) % TOK + xh * TOK
    col = lax.broadcasted_iota(jnp.int32, (rows, TOK), 1)
    col_tok = col // 32 * 64 + col % 32
    lane = lax.broadcasted_iota(jnp.int32, (rows, LANES), 1)
    causal = [jnp.where(col_tok + 32 * half <= row_tok, 0.0, NEG).astype(f32) for half in range(2)]
    for chunk in range(4):
        q = load_query(joint, chunk * rows, rows)
        scores = []
        for part in range(chunk + 1):
            for half in range(2):
                s = dot_t(q[half], keys[part, half].reshape(TOK, 640))
                if part == chunk:
                    s = s + causal[half]
                scores.append(s)
        top = functools.reduce(jnp.maximum, [jnp.max(s, -1, keepdims=True) for s in scores])
        expo = [jnp.exp2((s - top) * EXP_SCALE) for s in scores]
        denom = functools.reduce(jnp.add, [jnp.sum(e, -1, keepdims=True) for e in expo])
        weights = jnp.concatenate([e.astype(bf16) for e in expo], axis=1)
        total = dot(weights, keys[0 : chunk + 1, :, :, :, 0:512].reshape((chunk + 1) * rows, 512))
        stats_out[:, chunk * rows : (chunk + 1) * rows] = jnp.where(lane == 0, top, denom).T[0:8]
        mixed = (total / denom).astype(bf16)
        for h in range(2):
            part_out[chunk, :, h * 128 : (h + 1) * 128] = project(
                mixed[h * TOK : (h + 1) * TOK], value_up, core, h
            )


def prepare_kernel(q0, q1, q2, q3, key_up, joint, query, sems):
    (core,) = coords("core")
    for c in gather_query((q0, q1, q2, q3), query, sems):
        c.wait()
    pad = jnp.zeros((TOK, 64), bf16)
    for chunk in range(4):
        for h in range(2):
            rows = pl.ds((2 * chunk + h) * TOK, TOK)
            nope = query[chunk, :, h * 128 : (h + 1) * 128]
            pos = query[chunk, :, 256 + h * 64 : 256 + (h + 1) * 64]
            for i, cols in enumerate(halves(core)):
                joint[rows, i * 256 : (i + 1) * 256] = dot(nope, key_up[h, :, cols]).astype(bf16)
            pos = jnp.where(core == 0, pos, jnp.concatenate([pos[:, 32:64], pos[:, 0:32]], axis=1))
            joint[rows, 512:640] = jnp.concatenate([pos, pad], axis=1)


def cached_kernel(cached_len, joint, value_up, own, other, stats, new_part, token, out, keys):
    core, seq = coords("core", "y")
    span = PICK_LAT // 4
    pad = jnp.zeros((span, 64), bf16)
    for x in range(4):
        for i, ref in enumerate((own, other)):
            for zp in range(2):
                for e in range(4):
                    start = (e * 4 + x) * span
                    keys[start : start + span, (2 * i + zp) * LANES : (2 * i + zp + 1) * LANES] = ref[
                        x % 2, x // 2, zp, e * span : (e + 1) * span, :
                    ]
        packed = [
            jnp.concatenate([ref[x % 2, x // 2, zp, PICK_LAT:PICK_ROWS, :] for zp in range(2)], axis=0)
            for ref in (own, other)
        ]
        for e in range(4):
            start = (e * 4 + x) * span
            lanes = slice(32 * e, 32 * e + 32)
            keys[start : start + span, 512:640] = jnp.concatenate(
                [packed[0][:, lanes], packed[1][:, lanes], pad], axis=1
            )
    count = 16 * span
    index = lax.broadcasted_iota(jnp.int32, (1, count), 1)
    rest = index % span
    position = (index // (4 * span) * (BLOCKS // 4) + rest // PIECE) * 64
    position = position + index // span % 4 * PIECE + rest % PIECE
    length = cached_len[seq]
    bias = jnp.where(position < length, 0.0, NEG).astype(f32)
    rows = 4 * TOK
    for group in range(2):
        at = slice(group * rows, (group + 1) * rows)
        scores = dot_t(joint[at, :], keys[...]) + bias
        state = jnp.concatenate([stats[:, at]] * 16, axis=0).T
        before, denom_before = state[:, 0:1], state[:, 1:2]
        top = jnp.maximum(before, jnp.max(scores, -1, keepdims=True))
        factor = jnp.exp2((before - top) * EXP_SCALE) * denom_before
        expo = jnp.exp2((scores - top) * EXP_SCALE)
        denom = factor + jnp.sum(expo, -1, keepdims=True)
        total = dot(expo.astype(bf16), keys[:, 0:512])
        share = factor / denom
        mixed = (total / denom).astype(bf16)
        for c in range(2):
            chunk = group * 2 + c
            for h in range(2):
                tok = slice((2 * c + h) * TOK, (2 * c + h + 1) * TOK)
                cols = slice(h * 128, (h + 1) * 128)
                fresh = project(mixed[tok], value_up, core, h)
                out[chunk, :, cols] = (fresh + new_part[chunk, :, cols] * share[tok]).astype(bf16)


def smem():
    return pl.BlockSpec(memory_space=pltpu.SMEM)


def vmem():
    return pl.BlockSpec(memory_space=pltpu.VMEM)


def anywhere():
    return pl.BlockSpec(memory_space=pl.ANY)


def params(mib):
    return pltpu.CompilerParams(vmem_limit_bytes=mib * MIB)


def shape(dims, kind=bf16):
    return jax.ShapeDtypeStruct(dims, kind)


def on_device(
    query_nope,
    query_rope,
    key_up,
    value_up,
    new_latent,
    new_rope,
    cache_latent,
    cache_rope,
    block_owner,
    block_slot,
    cached_len,
):
    y = lax.axis_index("y")
    send = pl.pallas_call(
        pack_kernel,
        out_shape=shape((4, SEQS, MSG_ROWS, LANES)),
        in_specs=[anywhere()] * 6,
        out_specs=anywhere(),
        scratch_shapes=[
            pltpu.SMEM((SEQS, BLOCKS), jnp.int32),
            pltpu.SMEM((SEQS, BLOCKS), jnp.int32),
            pltpu.SMEM((16,), jnp.int32),
            pltpu.VMEM((32, 64, LANES), bf16),
            pltpu.VMEM((32, 64, 64), bf16),
            pltpu.VMEM((SEQS, 64, 2 * LANES), bf16),
            pltpu.VMEM((SEQS, 64, TOK), bf16),
            pltpu.VMEM((SEQS, TOK, 64), bf16),
            pltpu.VMEM((4, NEW_AT, LANES), bf16),
            pltpu.VMEM((SEQS, NEW_ROWS, LANES), bf16),
            pltpu.SemaphoreType.DMA((6,)),
            pltpu.SemaphoreType.DMA((8,)),
        ],
        compiler_params=params(63),
        name="pack",
    )(block_owner, block_slot, cache_latent, cache_rope, new_latent, jnp.swapaxes(new_rope, 1, 2))
    send, query_nope, query_rope, owner = lax.optimization_barrier(
        (send, query_nope, query_rope, block_owner)
    )
    plan = pl.pallas_call(
        plan_kernel,
        out_shape=shape((SEQS, BLOCKS), jnp.int32),
        in_specs=[smem()],
        out_specs=smem(),
        name="plan",
    )(owner)
    recv = lax.all_to_all(send.reshape(16, MSG_ROWS, LANES), PLANE, 0, 0)
    query = jnp.concatenate([query_nope, query_rope], -1)
    queries = []
    for k in range(4):
        part = lax.dynamic_index_in_dim(query, lax.rem(y + k, 4), 0, keepdims=False)
        if k == 3:
            part, plan = lax.optimization_barrier((part, plan))
        if k:
            part = lax.ppermute(part, "y", [(i, (i + k) % 4) for i in range(4)])
        queries.append(part)
    picked, new_own = pl.pallas_call(
        select_kernel,
        out_shape=(shape((8, PICK_ROWS, LANES)), shape((16, NEW_ROWS, LANES))),
        in_specs=[smem(), anywhere()],
        out_specs=(anywhere(), anywhere()),
        scratch_shapes=[
            pltpu.VMEM((16, NEW_AT, LANES), bf16),
            pltpu.VMEM((PICK_ROWS, LANES), bf16),
            pltpu.VMEM((BLOCKS // 4 * PIECE, LANES), bf16),
            pltpu.SemaphoreType.DMA((2,)),
            pltpu.SemaphoreType.DMA((8,)),
        ],
        compiler_params=params(16),
        name="select",
    )(plan, recv)
    picked, new_own, *queries = lax.optimization_barrier((picked, new_own, *queries))
    swap = [(0, 1), (1, 0)]
    new_own = new_own.reshape(2, 2, 4, NEW_ROWS, LANES)
    new_other = lax.ppermute(new_own, "core", swap)
    cache_own = lax.all_to_all(picked, SPREAD, 0, 0).reshape(2, 2, 2, PICK_ROWS, LANES)

    rows = 8 * TOK
    stats, part, token = pl.pallas_call(
        new_kernel,
        out_shape=(
            shape((8, rows), f32),
            shape((4, TOK, 256), f32),
            shape((8, LANES), f32),
        ),
        in_specs=[anywhere()] * 4 + [vmem()] * 4,
        out_specs=(vmem(),) * 3,
        scratch_shapes=[
            pltpu.VMEM((4, TOK, 384), bf16),
            pltpu.VMEM((rows, 768), bf16),
            pltpu.VMEM((4, 2, 4, 32, 640), bf16),
            pltpu.SemaphoreType.DMA((4,)),
        ],
        compiler_params=params(24),
        cost_estimate=pl.CostEstimate(flops=3 * 10**9, bytes_accessed=5 * 10**6, transcendentals=700000),
        name="attend_new",
    )(*queries, key_up, value_up, new_own, new_other)
    cache_own, token, *queries = lax.optimization_barrier((cache_own, token, *queries))
    cache_other = lax.ppermute(cache_own, "core", swap)
    joint = pl.pallas_call(
        prepare_kernel,
        out_shape=shape((rows, 640)),
        in_specs=[anywhere()] * 4 + [vmem()],
        out_specs=vmem(),
        scratch_shapes=[pltpu.VMEM((4, TOK, 384), bf16), pltpu.SemaphoreType.DMA((4,))],
        compiler_params=params(16),
        cost_estimate=pl.CostEstimate(flops=2 * 10**8, bytes_accessed=2 * 10**6, transcendentals=0),
        name="prepare",
    )(*queries, key_up)
    mixed = pl.pallas_call(
        cached_kernel,
        out_shape=shape((4, TOK, 256)),
        in_specs=[smem()] + [vmem()] * 7,
        out_specs=vmem(),
        scratch_shapes=[
            pltpu.VMEM((4 * PICK_LAT, 640), bf16),
        ],
        compiler_params=params(24),
        cost_estimate=pl.CostEstimate(flops=4 * 10**9, bytes_accessed=5 * 10**6, transcendentals=1600000),
        name="attend_cached",
    )(cached_len, joint, value_up, cache_own, cache_other, stats, part, token)
    return lax.all_to_all(mixed, "y", 0, 0)


def solution(mesh):
    fine = Mesh(
        mesh.devices.reshape(4, 2, 8, 2, 2, 2), ("y", "xh", "zh", "zp", "core", "xl")
    )
    ctx = ("y", "xh")
    heads = ("zh", "zp", "core", "xl")
    holders = ("y", "xh", "xl")
    return jax.shard_map(
        on_device,
        mesh=fine,
        in_specs=(
            P(None, ctx, heads),
            P(None, ctx, heads),
            P(heads, None, None),
            P(heads, None, None),
            P(None, ctx, None),
            P(None, ctx, None),
            P(holders, None, None),
            P(holders, None, None),
            P(),
            P(),
            P(),
        ),
        out_specs=P(None, ctx, heads),
        check_vma=False,
    )
```

```python
import functools

import jax
import jax.numpy as jnp
from jax import lax
from jax.experimental import pallas as pl
from jax.experimental.pallas import tpu as pltpu
from jax.sharding import Mesh
from jax.sharding import PartitionSpec as P

NEG = -1e30
LOG2E = 1.4426950408889634
EXP_SCALE = 192.0 ** (-0.5) * LOG2E
HOLDER = ("y", "xh", "xl")
PLANE = ("xh", "xl", "y")
SPREAD = ("zp", "xl", "xh")
CAP = 9
PIECE = 16
LANES = 128
SEQS = 4
BLOCKS = 24
TOK = 128
LAT_ROWS = CAP * PIECE
ROPE_ROWS = (CAP + 3) // 4 * PIECE
NEW_AT = LAT_ROWS + ROPE_ROWS
NEW_ROWS = 2 * 64 + 16
MSG_ROWS = NEW_AT + NEW_ROWS
PICK_LAT = BLOCKS * PIECE
PICK_PART = BLOCKS // 4 * PIECE // 2
PICK_ROWS = PICK_LAT + PICK_PART
MIB = 1024 * 1024
bf16 = jnp.bfloat16
f32 = jnp.float32


def coords(*names):
    return [lax.axis_index(n) for n in names]


def pack_kernel(
    owner,
    slot,
    cache_latent,
    cache_rope,
    new_latent,
    new_rope,
    out,
    owners,
    places,
    slots,
    lat,
    rope,
    nlat,
    nrope_t,
    nrope,
    cached_part,
    new_part,
    sems,
    out_sems,
):
    holder, core, xl, zp = coords(HOLDER, "core", "xl", "zp")
    table_copies = [
        pltpu.make_async_copy(owner, owners, sems.at[4]),
        pltpu.make_async_copy(slot, places, sems.at[5]),
    ]
    for c in table_copies:
        c.start()
    cols = pl.ds(pl.multiple_of((core * 2 + zp) * LANES, LANES), LANES)
    half = pl.ds(pl.multiple_of(core * 2 * LANES, 2 * LANES), 2 * LANES)
    rows = pl.ds(pl.multiple_of(xl * 64, 64), 64)
    new_copies = [
        pltpu.make_async_copy(new_latent.at[:, rows, half], nlat, sems.at[0]),
        pltpu.make_async_copy(new_rope, nrope_t, sems.at[1]),
    ]
    pool_copies = [
        pltpu.make_async_copy(cache_latent.at[:, :, cols], lat, sems.at[2]),
        pltpu.make_async_copy(cache_rope, rope, sems.at[3]),
    ]
    for c in new_copies + pool_copies:
        c.start()
    for r in range(CAP):
        slots[r] = 0
    for c in table_copies:
        c.wait()
    count = jnp.int32(0)
    for s in range(SEQS):
        for j in range(BLOCKS):
            hit = owners[s, j] == holder
            slots[jnp.where(hit, jnp.minimum(count, CAP), CAP)] = places[s, j]
            count = count + hit.astype(jnp.int32)
    for c in new_copies:
        c.wait()
    low = pl.ds(pl.multiple_of(xl * 64 + core * 16, 16), 16)
    high = pl.ds(pl.multiple_of(xl * 64 + 32 + core * 16, 16), 16)
    for s in range(SEQS):
        nrope[s] = nrope_t[s].T
        new_part[s, 0:64, :] = nlat[s, :, 0:LANES]
        new_part[s, 64:128, :] = nlat[s, :, LANES : 2 * LANES]
        new_part[s, 128:144, :] = jnp.concatenate([nrope[s, low, :], nrope[s, high, :]], axis=1)
    out_copies = [
        pltpu.make_async_copy(new_part, out.at[x, :, pl.ds(NEW_AT, NEW_ROWS), :], out_sems.at[x])
        for x in range(4)
    ]
    for c in out_copies:
        c.start()
    for c in pool_copies:
        c.wait()
    blocks = [slots[r] for r in range(CAP)]
    for r in range(CAP):
        for x in range(4):
            cached_part[x, r * PIECE : (r + 1) * PIECE, :] = lat[blocks[r], x * PIECE : (x + 1) * PIECE, :]
    for m in range((CAP + 3) // 4):
        quarter = []
        for r in range(4 * m, 4 * m + 4):
            whole = rope[blocks[min(r, CAP - 1)]]
            quarter.append(jnp.where(core == 0, whole[:, 0:32], whole[:, 32:64]))
        both = jnp.concatenate(quarter, axis=1)
        for x in range(4):
            cached_part[x, LAT_ROWS + m * PIECE : LAT_ROWS + (m + 1) * PIECE, :] = both[
                x * PIECE : (x + 1) * PIECE, :
            ]
    for s in range(SEQS):
        c = pltpu.make_async_copy(cached_part, out.at[:, s, pl.ds(0, NEW_AT), :], out_sems.at[4 + s])
        c.start()
        out_copies.append(c)
    for c in out_copies:
        c.wait()


def select_kernel(owner, recv, out, new_out, counts, cached, picked, packed, sems, out_sems):
    zp, seq = coords("zp", "y")
    arrive = pltpu.make_async_copy(recv.at[:, pl.ds(0, NEW_AT), :], cached, sems.at[0])
    arrive.start()
    new_copy = pltpu.make_async_copy(
        recv.at[:, pl.ds(NEW_AT, NEW_ROWS), :], new_out, sems.at[1]
    )
    new_copy.start()
    for h in range(16):
        counts[h] = 0

    def scan(s, carry):
        for j in range(BLOCKS):
            h = owner[s, j]
            counts[h] = counts[h] + 1
        return carry

    lax.fori_loop(0, seq, scan, jnp.int32(0))
    ranks, sources = [], []
    for j in range(BLOCKS):
        h = owner[seq, j]
        rank = counts[h]
        counts[h] = rank + 1
        ranks.append(jnp.minimum(rank, CAP - 1))
        sources.append((h & 3) * 4 + (h >> 2))
    arrive.wait()
    for j in range(BLOCKS):
        rows = pl.ds(pl.multiple_of(ranks[j] * PIECE, PIECE), PIECE)
        picked[j * PIECE : (j + 1) * PIECE, :] = cached[sources[j], rows, :]

    def rotary(j):
        rows = pl.ds(pl.multiple_of(LAT_ROWS + (ranks[j] >> 2) * PIECE, PIECE), PIECE)
        tile = cached[sources[j], rows, :]
        odd = (ranks[j] & 1) == 1
        left = jnp.where(odd, tile[:, 32:64], tile[:, 0:32])
        right = jnp.where(odd, tile[:, 96:128], tile[:, 64:96])
        return jnp.where((ranks[j] & 2) == 2, right, left)

    for j in range(BLOCKS // 4):
        packed[j * PIECE : (j + 1) * PIECE, :] = jnp.concatenate(
            [rotary(j + e * BLOCKS // 4) for e in range(4)], axis=1
        )
    picked[PICK_LAT:PICK_ROWS, :] = packed[pl.ds(pl.multiple_of(zp * PICK_PART, 16), PICK_PART), :]
    out_copies = [pltpu.make_async_copy(picked, out.at[d], out_sems.at[d]) for d in range(8)]
    for c in out_copies:
        c.start()
    for c in out_copies + [new_copy]:
        c.wait()


def dot(a, b):
    return lax.dot_general(a, b, (((1,), (0,)), ((), ())), preferred_element_type=f32)


def dot_t(a, b):
    return lax.dot_general(a, b, (((1,), (1,)), ((), ())), preferred_element_type=f32)


def gather_query(refs, query, sems):
    (y,) = coords("y")
    copies = []
    for k in range(4):
        at = lax.rem(y + 4 - k, 4)
        copies.append(pltpu.make_async_copy(refs[k], query.at[at], sems.at[k]))
    for c in copies:
        c.start()
    return copies


def halves(core):
    return [pl.ds(pl.multiple_of(c * 256, 256), 256) for c in (core, 1 - core)]


def joint_query(query, key_up, core, chunk, joint):
    pad = jnp.zeros((TOK, 64), bf16)
    for h in range(2):
        rows = pl.ds((2 * chunk + h) * TOK, TOK)
        nope = query[chunk, :, h * 128 : (h + 1) * 128]
        pos = query[chunk, :, 256 + h * 64 : 256 + (h + 1) * 64]
        for i, cols in enumerate(halves(core)):
            joint[rows, i * 256 : (i + 1) * 256] = dot(nope, key_up[h, :, cols]).astype(bf16)
        joint[rows, 512:640] = jnp.concatenate([pos, pad], axis=1)
        joint[rows, 640:768] = jnp.concatenate([pad, pos], axis=1)


def load_query(joint, start, count):
    low = joint[start : start + count, 0:640]
    high = jnp.concatenate([joint[start : start + count, 0:512], joint[start : start + count, 640:768]], axis=1)
    return low, high


def project(mixed, value_up, core, h):
    own, other = halves(core)
    return dot(mixed[:, 0:256], value_up[h, own, :]) + dot(mixed[:, 256:512], value_up[h, other, :])


def new_kernel(
    q0, q1, q2, q3, key_up, value_up, own, other, stats_out, part_out, token, query, joint, keys, sems
):
    core, xh = coords("core", "xh")
    query_copies = gather_query((q0, q1, q2, q3), query, sems)
    token[...] = jnp.zeros_like(token)
    for i, (which, ref) in enumerate(((core, own), (1 - core, other))):
        rope_rows = pl.ds(pl.multiple_of(which * 16, 16), 16)
        for y in range(4):
            for part in range(4):
                for half in range(2):
                    for tile in range(2):
                        at = tile * 64 + half * 32
                        col = (2 * i + tile) * LANES
                        keys[y, half, part, :, col : col + LANES] = ref[part // 2, part % 2, y, at : at + 32, :]
                    keys[y, half, part, rope_rows, 512:640] = ref[part // 2, part % 2, y, 128:144, :]
    for c in query_copies:
        c.wait()
    for chunk in range(4):
        joint_query(query, key_up, core, chunk, joint)
    rows = 2 * TOK
    row_tok = lax.broadcasted_iota(jnp.int32, (rows, TOK), 0) % TOK + xh * TOK
    col = lax.broadcasted_iota(jnp.int32, (rows, TOK), 1)
    col_tok = col // 32 * 64 + col % 32
    lane = lax.broadcasted_iota(jnp.int32, (rows, LANES), 1)
    causal = [jnp.where(col_tok + 32 * half <= row_tok, 0.0, NEG).astype(f32) for half in range(2)]
    for chunk in range(4):
        q = load_query(joint, chunk * rows, rows)
        scores = []
        for part in range(chunk + 1):
            for half in range(2):
                s = dot_t(q[half], keys[part, half].reshape(TOK, 640))
                if part == chunk:
                    s = s + causal[half]
                scores.append(s)
        top = functools.reduce(jnp.maximum, [jnp.max(s, -1, keepdims=True) for s in scores])
        expo = [jnp.exp2((s - top) * EXP_SCALE) for s in scores]
        denom = functools.reduce(jnp.add, [jnp.sum(e, -1, keepdims=True) for e in expo])
        weights = jnp.concatenate([e.astype(bf16) for e in expo], axis=1)
        total = dot(weights, keys[0 : chunk + 1, :, :, :, 0:512].reshape((chunk + 1) * rows, 512))
        stats_out[:, chunk * rows : (chunk + 1) * rows] = jnp.where(lane == 0, top, denom).T[0:8]
        mixed = (total / denom).astype(bf16)
        for h in range(2):
            part_out[chunk, :, h * 128 : (h + 1) * 128] = project(
                mixed[h * TOK : (h + 1) * TOK], value_up, core, h
            )


def prepare_kernel(q0, q1, q2, q3, key_up, joint, query, sems):
    (core,) = coords("core")
    for c in gather_query((q0, q1, q2, q3), query, sems):
        c.wait()
    pad = jnp.zeros((TOK, 64), bf16)
    for chunk in range(4):
        for h in range(2):
            rows = pl.ds((2 * chunk + h) * TOK, TOK)
            nope = query[chunk, :, h * 128 : (h + 1) * 128]
            pos = query[chunk, :, 256 + h * 64 : 256 + (h + 1) * 64]
            for i, cols in enumerate(halves(core)):
                joint[rows, i * 256 : (i + 1) * 256] = dot(nope, key_up[h, :, cols]).astype(bf16)
            pos = jnp.where(core == 0, pos, jnp.concatenate([pos[:, 32:64], pos[:, 0:32]], axis=1))
            joint[rows, 512:640] = jnp.concatenate([pos, pad], axis=1)


def cached_kernel(cached_len, joint, value_up, own, other, stats, new_part, token, out, keys):
    core, seq = coords("core", "y")
    span = PICK_LAT // 4
    pad = jnp.zeros((span, 64), bf16)
    for x in range(4):
        for i, ref in enumerate((own, other)):
            for zp in range(2):
                for e in range(4):
                    start = (e * 4 + x) * span
                    keys[start : start + span, (2 * i + zp) * LANES : (2 * i + zp + 1) * LANES] = ref[
                        zp, x % 2, x // 2, e * span : (e + 1) * span, :
                    ]
        packed = [
            jnp.concatenate([ref[zp, x % 2, x // 2, PICK_LAT:PICK_ROWS, :] for zp in range(2)], axis=0)
            for ref in (own, other)
        ]
        for e in range(4):
            start = (e * 4 + x) * span
            lanes = slice(32 * e, 32 * e + 32)
            keys[start : start + span, 512:640] = jnp.concatenate(
                [packed[0][:, lanes], packed[1][:, lanes], pad], axis=1
            )
    count = 16 * span
    index = lax.broadcasted_iota(jnp.int32, (1, count), 1)
    rest = index % span
    position = (index // (4 * span) * (BLOCKS // 4) + rest // PIECE) * 64
    position = position + index // span % 4 * PIECE + rest % PIECE
    length = cached_len[seq]
    bias = jnp.where(position < length, 0.0, NEG).astype(f32)
    rows = 4 * TOK
    for group in range(2):
        at = slice(group * rows, (group + 1) * rows)
        scores = dot_t(joint[at, :], keys[...]) + bias
        state = jnp.concatenate([stats[:, at]] * 16, axis=0).T
        before, denom_before = state[:, 0:1], state[:, 1:2]
        top = jnp.maximum(before, jnp.max(scores, -1, keepdims=True))
        factor = jnp.exp2((before - top) * EXP_SCALE) * denom_before
        expo = jnp.exp2((scores - top) * EXP_SCALE)
        denom = factor + jnp.sum(expo, -1, keepdims=True)
        total = dot(expo.astype(bf16), keys[:, 0:512])
        share = factor / denom
        mixed = (total / denom).astype(bf16)
        for c in range(2):
            chunk = group * 2 + c
            for h in range(2):
                tok = slice((2 * c + h) * TOK, (2 * c + h + 1) * TOK)
                cols = slice(h * 128, (h + 1) * 128)
                fresh = project(mixed[tok], value_up, core, h)
                out[chunk, :, cols] = (fresh + new_part[chunk, :, cols] * share[tok]).astype(bf16)


def smem():
    return pl.BlockSpec(memory_space=pltpu.SMEM)


def vmem():
    return pl.BlockSpec(memory_space=pltpu.VMEM)


def anywhere():
    return pl.BlockSpec(memory_space=pl.ANY)


def params(mib):
    return pltpu.CompilerParams(vmem_limit_bytes=mib * MIB)


def shape(dims, kind=bf16):
    return jax.ShapeDtypeStruct(dims, kind)


def on_device(
    query_nope,
    query_rope,
    key_up,
    value_up,
    new_latent,
    new_rope,
    cache_latent,
    cache_rope,
    block_owner,
    block_slot,
    cached_len,
):
    y = lax.axis_index("y")
    send = pl.pallas_call(
        pack_kernel,
        out_shape=shape((4, SEQS, MSG_ROWS, LANES)),
        in_specs=[anywhere()] * 6,
        out_specs=anywhere(),
        scratch_shapes=[
            pltpu.SMEM((SEQS, BLOCKS), jnp.int32),
            pltpu.SMEM((SEQS, BLOCKS), jnp.int32),
            pltpu.SMEM((16,), jnp.int32),
            pltpu.VMEM((32, 64, LANES), bf16),
            pltpu.VMEM((32, 64, 64), bf16),
            pltpu.VMEM((SEQS, 64, 2 * LANES), bf16),
            pltpu.VMEM((SEQS, 64, TOK), bf16),
            pltpu.VMEM((SEQS, TOK, 64), bf16),
            pltpu.VMEM((4, NEW_AT, LANES), bf16),
            pltpu.VMEM((SEQS, NEW_ROWS, LANES), bf16),
            pltpu.SemaphoreType.DMA((6,)),
            pltpu.SemaphoreType.DMA((8,)),
        ],
        compiler_params=params(63),
        name="pack",
    )(block_owner, block_slot, cache_latent, cache_rope, new_latent, jnp.swapaxes(new_rope, 1, 2))
    send, query_nope, query_rope = lax.optimization_barrier((send, query_nope, query_rope))
    recv = lax.all_to_all(send.reshape(16, MSG_ROWS, LANES), PLANE, 0, 0)
    query = jnp.concatenate([query_nope, query_rope], -1)
    queries = []
    for k in range(4):
        part = lax.dynamic_index_in_dim(query, lax.rem(y + k, 4), 0, keepdims=False)
        if k:
            part = lax.ppermute(part, "y", [(i, (i + k) % 4) for i in range(4)])
        queries.append(part)
    picked, new_own = pl.pallas_call(
        select_kernel,
        out_shape=(shape((8, PICK_ROWS, LANES)), shape((16, NEW_ROWS, LANES))),
        in_specs=[smem(), anywhere()],
        out_specs=(anywhere(), anywhere()),
        scratch_shapes=[
            pltpu.SMEM((16,), jnp.int32),
            pltpu.VMEM((16, NEW_AT, LANES), bf16),
            pltpu.VMEM((PICK_ROWS, LANES), bf16),
            pltpu.VMEM((BLOCKS // 4 * PIECE, LANES), bf16),
            pltpu.SemaphoreType.DMA((2,)),
            pltpu.SemaphoreType.DMA((8,)),
        ],
        compiler_params=params(16),
        name="select",
    )(block_owner, recv)
    picked, new_own, *queries = lax.optimization_barrier((picked, new_own, *queries))
    swap = [(0, 1), (1, 0)]
    new_own = new_own.reshape(2, 2, 4, NEW_ROWS, LANES)
    new_other = lax.ppermute(new_own, "core", swap)
    cache_own = lax.all_to_all(picked, SPREAD, 0, 0).reshape(2, 2, 2, PICK_ROWS, LANES)

    rows = 8 * TOK
    stats, part, token = pl.pallas_call(
        new_kernel,
        out_shape=(
            shape((8, rows), f32),
            shape((4, TOK, 256), f32),
            shape((8, LANES), f32),
        ),
        in_specs=[anywhere()] * 4 + [vmem()] * 4,
        out_specs=(vmem(),) * 3,
        scratch_shapes=[
            pltpu.VMEM((4, TOK, 384), bf16),
            pltpu.VMEM((rows, 768), bf16),
            pltpu.VMEM((4, 2, 4, 32, 640), bf16),
            pltpu.SemaphoreType.DMA((4,)),
        ],
        compiler_params=params(24),
        cost_estimate=pl.CostEstimate(flops=3 * 10**9, bytes_accessed=5 * 10**6, transcendentals=700000),
        name="attend_new",
    )(*queries, key_up, value_up, new_own, new_other)
    cache_own, token, *queries = lax.optimization_barrier((cache_own, token, *queries))
    cache_other = lax.ppermute(cache_own, "core", swap)
    joint = pl.pallas_call(
        prepare_kernel,
        out_shape=shape((rows, 640)),
        in_specs=[anywhere()] * 4 + [vmem()],
        out_specs=vmem(),
        scratch_shapes=[pltpu.VMEM((4, TOK, 384), bf16), pltpu.SemaphoreType.DMA((4,))],
        compiler_params=params(16),
        cost_estimate=pl.CostEstimate(flops=2 * 10**8, bytes_accessed=2 * 10**6, transcendentals=0),
        name="prepare",
    )(*queries, key_up)
    mixed = pl.pallas_call(
        cached_kernel,
        out_shape=shape((4, TOK, 256)),
        in_specs=[smem()] + [vmem()] * 7,
        out_specs=vmem(),
        scratch_shapes=[
            pltpu.VMEM((4 * PICK_LAT, 640), bf16),
        ],
        compiler_params=params(24),
        cost_estimate=pl.CostEstimate(flops=4 * 10**9, bytes_accessed=5 * 10**6, transcendentals=1600000),
        name="attend_cached",
    )(cached_len, joint, value_up, cache_own, cache_other, stats, part, token)
    return lax.all_to_all(mixed, "y", 0, 0)


def solution(mesh):
    fine = Mesh(
        mesh.devices.reshape(4, 2, 8, 2, 2, 2), ("y", "xh", "zh", "zp", "core", "xl")
    )
    ctx = ("y", "xh")
    heads = ("zh", "zp", "core", "xl")
    holders = ("y", "xh", "xl")
    return jax.shard_map(
        on_device,
        mesh=fine,
        in_specs=(
            P(None, ctx, heads),
            P(None, ctx, heads),
            P(heads, None, None),
            P(heads, None, None),
            P(None, ctx, None),
            P(None, ctx, None),
            P(holders, None, None),
            P(holders, None, None),
            P(),
            P(),
            P(),
        ),
        out_specs=P(None, ctx, heads),
        check_vma=False,
    )
```

```python
import functools

import jax
import jax.numpy as jnp
from jax import lax
from jax.experimental import pallas as pl
from jax.experimental.pallas import tpu as pltpu
from jax.sharding import Mesh
from jax.sharding import PartitionSpec as P

NEG = -1e30
LOG2E = 1.4426950408889634
EXP_SCALE = 192.0 ** (-0.5) * LOG2E
HOLDER = ("y", "xh", "xl")
PLANE = ("xh", "xl", "y")
SPREAD = ("zp", "xl", "xh")
CAP = 9
PIECE = 16
LANES = 128
SEQS = 4
BLOCKS = 24
TOK = 128
LAT_ROWS = CAP * PIECE
ROPE_ROWS = (CAP + 3) // 4 * PIECE
NEW_AT = LAT_ROWS + ROPE_ROWS
NEW_ROWS = 2 * 64 + 16
MSG_ROWS = NEW_AT + NEW_ROWS
PICK_LAT = BLOCKS * PIECE
PICK_PART = BLOCKS // 4 * PIECE // 2
PICK_ROWS = PICK_LAT + PICK_PART
MIB = 1024 * 1024
bf16 = jnp.bfloat16
f32 = jnp.float32


def coords(*names):
    return [lax.axis_index(n) for n in names]


def pack_kernel(
    owner,
    slot,
    cache_latent,
    cache_rope,
    new_latent,
    new_rope,
    out,
    owners,
    places,
    slots,
    lat,
    rope,
    nlat,
    nrope_t,
    nrope,
    cached_part,
    new_part,
    sems,
    out_sems,
):
    holder, core, xl, zp = coords(HOLDER, "core", "xl", "zp")
    table_copies = [
        pltpu.make_async_copy(owner, owners, sems.at[4]),
        pltpu.make_async_copy(slot, places, sems.at[5]),
    ]
    for c in table_copies:
        c.start()
    cols = pl.ds(pl.multiple_of((core * 2 + zp) * LANES, LANES), LANES)
    half = pl.ds(pl.multiple_of(core * 2 * LANES, 2 * LANES), 2 * LANES)
    rows = pl.ds(pl.multiple_of(xl * 64, 64), 64)
    new_copies = [
        pltpu.make_async_copy(new_latent.at[:, rows, half], nlat, sems.at[0]),
        pltpu.make_async_copy(new_rope, nrope_t, sems.at[1]),
    ]
    pool_copies = [
        pltpu.make_async_copy(cache_latent.at[:, :, cols], lat, sems.at[2]),
        pltpu.make_async_copy(cache_rope, rope, sems.at[3]),
    ]
    for c in new_copies + pool_copies:
        c.start()
    for r in range(CAP):
        slots[r] = 0
    for c in table_copies:
        c.wait()
    count = jnp.int32(0)
    for s in range(SEQS):
        for j in range(BLOCKS):
            hit = owners[s, j] == holder
            slots[jnp.where(hit, jnp.minimum(count, CAP), CAP)] = places[s, j]
            count = count + hit.astype(jnp.int32)
    for c in new_copies:
        c.wait()
    low = pl.ds(pl.multiple_of(xl * 64 + core * 16, 16), 16)
    high = pl.ds(pl.multiple_of(xl * 64 + 32 + core * 16, 16), 16)
    for s in range(SEQS):
        nrope[s] = nrope_t[s].T
        new_part[s, 0:64, :] = nlat[s, :, 0:LANES]
        new_part[s, 64:128, :] = nlat[s, :, LANES : 2 * LANES]
        new_part[s, 128:144, :] = jnp.concatenate([nrope[s, low, :], nrope[s, high, :]], axis=1)
    out_copies = [
        pltpu.make_async_copy(new_part, out.at[x, :, pl.ds(NEW_AT, NEW_ROWS), :], out_sems.at[x])
        for x in range(4)
    ]
    for c in out_copies:
        c.start()
    for c in pool_copies:
        c.wait()
    blocks = [slots[r] for r in range(CAP)]
    for r in range(CAP):
        for x in range(4):
            cached_part[x, r * PIECE : (r + 1) * PIECE, :] = lat[blocks[r], x * PIECE : (x + 1) * PIECE, :]
    for m in range((CAP + 3) // 4):
        quarter = []
        for r in range(4 * m, 4 * m + 4):
            whole = rope[blocks[min(r, CAP - 1)]]
            quarter.append(jnp.where(core == 0, whole[:, 0:32], whole[:, 32:64]))
        both = jnp.concatenate(quarter, axis=1)
        for x in range(4):
            cached_part[x, LAT_ROWS + m * PIECE : LAT_ROWS + (m + 1) * PIECE, :] = both[
                x * PIECE : (x + 1) * PIECE, :
            ]
    for s in range(SEQS):
        c = pltpu.make_async_copy(cached_part, out.at[:, s, pl.ds(0, NEW_AT), :], out_sems.at[4 + s])
        c.start()
        out_copies.append(c)
    for c in out_copies:
        c.wait()


def select_kernel(owner, recv, out, new_out, counts, cached, picked, packed, sems, out_sems):
    zp, seq = coords("zp", "y")
    arrive = pltpu.make_async_copy(recv.at[:, pl.ds(0, NEW_AT), :], cached, sems.at[0])
    arrive.start()
    new_copy = pltpu.make_async_copy(
        recv.at[:, pl.ds(NEW_AT, NEW_ROWS), :], new_out, sems.at[1]
    )
    new_copy.start()
    for h in range(16):
        counts[h] = 0

    def scan(s, carry):
        for j in range(BLOCKS):
            h = owner[s, j]
            counts[h] = counts[h] + 1
        return carry

    lax.fori_loop(0, seq, scan, jnp.int32(0))
    ranks, sources = [], []
    for j in range(BLOCKS):
        h = owner[seq, j]
        rank = counts[h]
        counts[h] = rank + 1
        ranks.append(jnp.minimum(rank, CAP - 1))
        sources.append((h & 3) * 4 + (h >> 2))
    arrive.wait()
    for j in range(BLOCKS):
        rows = pl.ds(pl.multiple_of(ranks[j] * PIECE, PIECE), PIECE)
        picked[j * PIECE : (j + 1) * PIECE, :] = cached[sources[j], rows, :]

    def rotary(j):
        rows = pl.ds(pl.multiple_of(LAT_ROWS + (ranks[j] >> 2) * PIECE, PIECE), PIECE)
        tile = cached[sources[j], rows, :]
        odd = (ranks[j] & 1) == 1
        left = jnp.where(odd, tile[:, 32:64], tile[:, 0:32])
        right = jnp.where(odd, tile[:, 96:128], tile[:, 64:96])
        return jnp.where((ranks[j] & 2) == 2, right, left)

    for j in range(BLOCKS // 4):
        packed[j * PIECE : (j + 1) * PIECE, :] = jnp.concatenate(
            [rotary(j + e * BLOCKS // 4) for e in range(4)], axis=1
        )
    picked[PICK_LAT:PICK_ROWS, :] = packed[pl.ds(pl.multiple_of(zp * PICK_PART, 16), PICK_PART), :]
    out_copies = [pltpu.make_async_copy(picked, out.at[d], out_sems.at[d]) for d in range(8)]
    for c in out_copies:
        c.start()
    for c in out_copies + [new_copy]:
        c.wait()


def dot(a, b):
    return lax.dot_general(a, b, (((1,), (0,)), ((), ())), preferred_element_type=f32)


def dot_t(a, b):
    return lax.dot_general(a, b, (((1,), (1,)), ((), ())), preferred_element_type=f32)


def gather_query(refs, query, sems):
    (y,) = coords("y")
    copies = []
    for k in range(4):
        at = lax.rem(y + 4 - k, 4)
        copies.append(pltpu.make_async_copy(refs[k], query.at[at], sems.at[k]))
    for c in copies:
        c.start()
    return copies


def halves(core):
    return [pl.ds(pl.multiple_of(c * 256, 256), 256) for c in (core, 1 - core)]


def joint_query(query, key_up, core, chunk, joint):
    pad = jnp.zeros((TOK, 64), bf16)
    for h in range(2):
        rows = pl.ds((2 * chunk + h) * TOK, TOK)
        nope = query[chunk, :, h * 128 : (h + 1) * 128]
        pos = query[chunk, :, 256 + h * 64 : 256 + (h + 1) * 64]
        for i, cols in enumerate(halves(core)):
            joint[rows, i * 256 : (i + 1) * 256] = dot(nope, key_up[h, :, cols]).astype(bf16)
        joint[rows, 512:640] = jnp.concatenate([pos, pad], axis=1)
        joint[rows, 640:768] = jnp.concatenate([pad, pos], axis=1)


def load_query(joint, start, count):
    low = joint[start : start + count, 0:640]
    high = jnp.concatenate([joint[start : start + count, 0:512], joint[start : start + count, 640:768]], axis=1)
    return low, high


def project(mixed, value_up, core, h):
    own, other = halves(core)
    return dot(mixed[:, 0:256], value_up[h, own, :]) + dot(mixed[:, 256:512], value_up[h, other, :])


def new_kernel(
    q0, q1, q2, q3, key_up, value_up, own, other, stats_out, part_out, token, query, joint, keys, sems
):
    core, xh = coords("core", "xh")
    query_copies = gather_query((q0, q1, q2, q3), query, sems)
    token[...] = jnp.zeros_like(token)
    for i, (which, ref) in enumerate(((core, own), (1 - core, other))):
        rope_rows = pl.ds(pl.multiple_of(which * 16, 16), 16)
        for y in range(4):
            for part in range(4):
                for half in range(2):
                    for tile in range(2):
                        at = tile * 64 + half * 32
                        col = (2 * i + tile) * LANES
                        keys[y, half, part, :, col : col + LANES] = ref[part // 2, part % 2, y, at : at + 32, :]
                    keys[y, half, part, rope_rows, 512:640] = ref[part // 2, part % 2, y, 128:144, :]
    for c in query_copies:
        c.wait()
    for chunk in range(4):
        joint_query(query, key_up, core, chunk, joint)
    rows = 2 * TOK
    row_tok = lax.broadcasted_iota(jnp.int32, (rows, TOK), 0) % TOK + xh * TOK
    col = lax.broadcasted_iota(jnp.int32, (rows, TOK), 1)
    col_tok = col // 32 * 64 + col % 32
    lane = lax.broadcasted_iota(jnp.int32, (rows, LANES), 1)
    causal = [jnp.where(col_tok + 32 * half <= row_tok, 0.0, NEG).astype(f32) for half in range(2)]
    for chunk in range(4):
        q = load_query(joint, chunk * rows, rows)
        scores = []
        for part in range(chunk + 1):
            for half in range(2):
                s = dot_t(q[half], keys[part, half].reshape(TOK, 640))
                if part == chunk:
                    s = s + causal[half]
                scores.append(s)
        top = functools.reduce(jnp.maximum, [jnp.max(s, -1, keepdims=True) for s in scores])
        expo = [jnp.exp2((s - top) * EXP_SCALE) for s in scores]
        denom = functools.reduce(jnp.add, [jnp.sum(e, -1, keepdims=True) for e in expo])
        weights = jnp.concatenate([e.astype(bf16) for e in expo], axis=1)
        total = dot(weights, keys[0 : chunk + 1, :, :, :, 0:512].reshape((chunk + 1) * rows, 512))
        stats_out[:, chunk * rows : (chunk + 1) * rows] = jnp.where(lane == 0, top, denom).T[0:8]
        mixed = (total / denom).astype(bf16)
        for h in range(2):
            part_out[chunk, :, h * 128 : (h + 1) * 128] = project(
                mixed[h * TOK : (h + 1) * TOK], value_up, core, h
            )


def prepare_kernel(q0, q1, q2, q3, key_up, joint, query, sems):
    (core,) = coords("core")
    for c in gather_query((q0, q1, q2, q3), query, sems):
        c.wait()
    pad = jnp.zeros((TOK, 64), bf16)
    for chunk in range(4):
        for h in range(2):
            rows = pl.ds((2 * chunk + h) * TOK, TOK)
            nope = query[chunk, :, h * 128 : (h + 1) * 128]
            pos = query[chunk, :, 256 + h * 64 : 256 + (h + 1) * 64]
            for i, cols in enumerate(halves(core)):
                joint[rows, i * 256 : (i + 1) * 256] = dot(nope, key_up[h, :, cols]).astype(bf16)
            pos = jnp.where(core == 0, pos, jnp.concatenate([pos[:, 32:64], pos[:, 0:32]], axis=1))
            joint[rows, 512:640] = jnp.concatenate([pos, pad], axis=1)


def cached_kernel(cached_len, joint, value_up, own, other, stats, new_part, token, out, keys):
    core, seq = coords("core", "y")
    span = PICK_LAT // 4
    pad = jnp.zeros((span, 64), bf16)
    packed = [
        [
            jnp.concatenate([ref[zp, x % 2, x // 2, PICK_LAT:PICK_ROWS, :] for zp in range(2)], axis=0)
            for ref in (own, other)
        ]
        for x in range(4)
    ]
    rows, count = 4 * TOK, 8 * span

    def assemble(half):
        for e in (2 * half, 2 * half + 1):
            for x in range(4):
                start = (e * 4 + x) * span
                for i, ref in enumerate((own, other)):
                    for zp in range(2):
                        keys[start : start + span, (2 * i + zp) * LANES : (2 * i + zp + 1) * LANES] = ref[
                            zp, x % 2, x // 2, e * span : (e + 1) * span, :
                        ]
                lanes = slice(32 * e, 32 * e + 32)
                keys[start : start + span, 512:640] = jnp.concatenate(
                    [packed[x][0][:, lanes], packed[x][1][:, lanes], pad], axis=1
                )

    length = cached_len[seq]
    index = lax.broadcasted_iota(jnp.int32, (1, 2 * count), 1)
    rest = index % span
    position = (index // (4 * span) * (BLOCKS // 4) + rest // PIECE) * 64
    position = position + index // span % 4 * PIECE + rest % PIECE
    bias = jnp.where(position < length, 0.0, NEG).astype(f32)

    def score(group, half):
        q = joint[group * rows : (group + 1) * rows, :]
        at = slice(half * count, (half + 1) * count)
        return dot_t(q, keys[at, :]) + bias[:, at]

    def soften(group, scores):
        state = jnp.concatenate([stats[:, group * rows : (group + 1) * rows]] * 16, axis=0).T
        before, denom_before = state[:, 0:1], state[:, 1:2]
        top = functools.reduce(jnp.maximum, [before] + [jnp.max(s, -1, keepdims=True) for s in scores])
        factor = jnp.exp2((before - top) * EXP_SCALE) * denom_before
        expo = [jnp.exp2((s - top) * EXP_SCALE) for s in scores]
        denom = functools.reduce(jnp.add, [factor] + [jnp.sum(e, -1, keepdims=True) for e in expo])
        weights = jnp.concatenate([e.astype(bf16) for e in expo], axis=1)
        return weights, denom, factor / denom

    def finish(group, weights, denom, share):
        mixed = (dot(weights, keys[:, 0:512]) / denom).astype(bf16)
        for c in range(2):
            chunk = group * 2 + c
            for h in range(2):
                tok = slice((2 * c + h) * TOK, (2 * c + h + 1) * TOK)
                cols = slice(h * 128, (h + 1) * 128)
                fresh = project(mixed[tok], value_up, core, h)
                out[chunk, :, cols] = (fresh + new_part[chunk, :, cols] * share[tok]).astype(bf16)

    assemble(0)
    first = [score(0, 0)]
    assemble(1)
    first.append(score(0, 1))
    second = [score(1, 0), score(1, 1)]
    first = soften(0, first)
    second = soften(1, second)
    finish(0, *first)
    finish(1, *second)


def smem():
    return pl.BlockSpec(memory_space=pltpu.SMEM)


def vmem():
    return pl.BlockSpec(memory_space=pltpu.VMEM)


def anywhere():
    return pl.BlockSpec(memory_space=pl.ANY)


def params(mib):
    return pltpu.CompilerParams(vmem_limit_bytes=mib * MIB)


def shape(dims, kind=bf16):
    return jax.ShapeDtypeStruct(dims, kind)


def on_device(
    query_nope,
    query_rope,
    key_up,
    value_up,
    new_latent,
    new_rope,
    cache_latent,
    cache_rope,
    block_owner,
    block_slot,
    cached_len,
):
    y = lax.axis_index("y")
    send = pl.pallas_call(
        pack_kernel,
        out_shape=shape((4, SEQS, MSG_ROWS, LANES)),
        in_specs=[anywhere()] * 6,
        out_specs=anywhere(),
        scratch_shapes=[
            pltpu.SMEM((SEQS, BLOCKS), jnp.int32),
            pltpu.SMEM((SEQS, BLOCKS), jnp.int32),
            pltpu.SMEM((16,), jnp.int32),
            pltpu.VMEM((32, 64, LANES), bf16),
            pltpu.VMEM((32, 64, 64), bf16),
            pltpu.VMEM((SEQS, 64, 2 * LANES), bf16),
            pltpu.VMEM((SEQS, 64, TOK), bf16),
            pltpu.VMEM((SEQS, TOK, 64), bf16),
            pltpu.VMEM((4, NEW_AT, LANES), bf16),
            pltpu.VMEM((SEQS, NEW_ROWS, LANES), bf16),
            pltpu.SemaphoreType.DMA((6,)),
            pltpu.SemaphoreType.DMA((8,)),
        ],
        compiler_params=params(63),
        name="pack",
    )(block_owner, block_slot, cache_latent, cache_rope, new_latent, jnp.swapaxes(new_rope, 1, 2))
    send, query_nope, query_rope = lax.optimization_barrier((send, query_nope, query_rope))
    recv = lax.all_to_all(send.reshape(16, MSG_ROWS, LANES), PLANE, 0, 0)
    query = jnp.concatenate([query_nope, query_rope], -1)
    queries = []
    for k in range(4):
        part = lax.dynamic_index_in_dim(query, lax.rem(y + k, 4), 0, keepdims=False)
        if k:
            part = lax.ppermute(part, "y", [(i, (i + k) % 4) for i in range(4)])
        queries.append(part)
    picked, new_own = pl.pallas_call(
        select_kernel,
        out_shape=(shape((8, PICK_ROWS, LANES)), shape((16, NEW_ROWS, LANES))),
        in_specs=[smem(), anywhere()],
        out_specs=(anywhere(), anywhere()),
        scratch_shapes=[
            pltpu.SMEM((16,), jnp.int32),
            pltpu.VMEM((16, NEW_AT, LANES), bf16),
            pltpu.VMEM((PICK_ROWS, LANES), bf16),
            pltpu.VMEM((BLOCKS // 4 * PIECE, LANES), bf16),
            pltpu.SemaphoreType.DMA((2,)),
            pltpu.SemaphoreType.DMA((8,)),
        ],
        compiler_params=params(16),
        name="select",
    )(block_owner, recv)
    picked, new_own, *queries = lax.optimization_barrier((picked, new_own, *queries))
    swap = [(0, 1), (1, 0)]
    new_own = new_own.reshape(2, 2, 4, NEW_ROWS, LANES)
    new_other = lax.ppermute(new_own, "core", swap)
    cache_own = lax.all_to_all(picked, SPREAD, 0, 0).reshape(2, 2, 2, PICK_ROWS, LANES)

    rows = 8 * TOK
    stats, part, token = pl.pallas_call(
        new_kernel,
        out_shape=(
            shape((8, rows), f32),
            shape((4, TOK, 256), f32),
            shape((8, LANES), f32),
        ),
        in_specs=[anywhere()] * 4 + [vmem()] * 4,
        out_specs=(vmem(),) * 3,
        scratch_shapes=[
            pltpu.VMEM((4, TOK, 384), bf16),
            pltpu.VMEM((rows, 768), bf16),
            pltpu.VMEM((4, 2, 4, 32, 640), bf16),
            pltpu.SemaphoreType.DMA((4,)),
        ],
        compiler_params=params(24),
        cost_estimate=pl.CostEstimate(flops=3 * 10**9, bytes_accessed=5 * 10**6, transcendentals=700000),
        name="attend_new",
    )(*queries, key_up, value_up, new_own, new_other)
    cache_own, token, *queries = lax.optimization_barrier((cache_own, token, *queries))
    cache_other = lax.ppermute(cache_own, "core", swap)
    joint = pl.pallas_call(
        prepare_kernel,
        out_shape=shape((rows, 640)),
        in_specs=[anywhere()] * 4 + [vmem()],
        out_specs=vmem(),
        scratch_shapes=[pltpu.VMEM((4, TOK, 384), bf16), pltpu.SemaphoreType.DMA((4,))],
        compiler_params=params(16),
        cost_estimate=pl.CostEstimate(flops=2 * 10**8, bytes_accessed=2 * 10**6, transcendentals=0),
        name="prepare",
    )(*queries, key_up)
    mixed = pl.pallas_call(
        cached_kernel,
        out_shape=shape((4, TOK, 256)),
        in_specs=[smem()] + [vmem()] * 7,
        out_specs=vmem(),
        scratch_shapes=[
            pltpu.VMEM((4 * PICK_LAT, 640), bf16),
        ],
        compiler_params=params(24),
        cost_estimate=pl.CostEstimate(flops=4 * 10**9, bytes_accessed=5 * 10**6, transcendentals=1600000),
        name="attend_cached",
    )(cached_len, joint, value_up, cache_own, cache_other, stats, part, token)
    return lax.all_to_all(mixed, "y", 0, 0)


def solution(mesh):
    fine = Mesh(
        mesh.devices.reshape(4, 2, 8, 2, 2, 2), ("y", "xh", "zh", "zp", "core", "xl")
    )
    ctx = ("y", "xh")
    heads = ("zh", "zp", "core", "xl")
    holders = ("y", "xh", "xl")
    return jax.shard_map(
        on_device,
        mesh=fine,
        in_specs=(
            P(None, ctx, heads),
            P(None, ctx, heads),
            P(heads, None, None),
            P(heads, None, None),
            P(None, ctx, None),
            P(None, ctx, None),
            P(holders, None, None),
            P(holders, None, None),
            P(),
            P(),
            P(),
        ),
        out_specs=P(None, ctx, heads),
        check_vma=False,
    )
```

```python
import functools

import jax
import jax.numpy as jnp
from jax import lax
from jax.experimental import pallas as pl
from jax.experimental.pallas import tpu as pltpu
from jax.sharding import Mesh
from jax.sharding import PartitionSpec as P

NEG = -1e30
LOG2E = 1.4426950408889634
EXP_SCALE = 192.0 ** (-0.5) * LOG2E
HOLDER = ("y", "xh", "xl")
PLANE = ("xh", "xl", "y")
SPREAD = ("zp", "xl", "xh")
CAP = 9
PIECE = 16
LANES = 128
SEQS = 4
BLOCKS = 24
TOK = 128
LAT_ROWS = CAP * PIECE
ROPE_ROWS = (CAP + 3) // 4 * PIECE
NEW_AT = LAT_ROWS + ROPE_ROWS
NEW_ROWS = 2 * 64 + 16
MSG_ROWS = NEW_AT + NEW_ROWS
PICK_LAT = BLOCKS * PIECE
PICK_PART = BLOCKS // 4 * PIECE // 2
PICK_ROWS = PICK_LAT + PICK_PART
MIB = 1024 * 1024
bf16 = jnp.bfloat16
f32 = jnp.float32


def coords(*names):
    return [lax.axis_index(n) for n in names]


def pack_kernel(
    owner,
    slot,
    cache_latent,
    cache_rope,
    new_latent,
    new_rope,
    out,
    owners,
    places,
    slots,
    lat,
    rope,
    nlat,
    nrope_t,
    nrope,
    cached_part,
    new_part,
    sems,
    out_sems,
):
    holder, core, xl, zp = coords(HOLDER, "core", "xl", "zp")
    table_copies = [
        pltpu.make_async_copy(owner, owners, sems.at[4]),
        pltpu.make_async_copy(slot, places, sems.at[5]),
    ]
    for c in table_copies:
        c.start()
    cols = pl.ds(pl.multiple_of((core * 2 + zp) * LANES, LANES), LANES)
    half = pl.ds(pl.multiple_of(core * 2 * LANES, 2 * LANES), 2 * LANES)
    rows = pl.ds(pl.multiple_of(xl * 64, 64), 64)
    new_copies = [
        pltpu.make_async_copy(new_latent.at[:, rows, half], nlat, sems.at[0]),
        pltpu.make_async_copy(new_rope, nrope_t, sems.at[1]),
    ]
    pool_copies = [
        pltpu.make_async_copy(cache_latent.at[:, :, cols], lat, sems.at[2]),
        pltpu.make_async_copy(cache_rope, rope, sems.at[3]),
    ]
    for c in new_copies + pool_copies:
        c.start()
    for r in range(CAP):
        slots[r] = 0
    for c in table_copies:
        c.wait()
    count = jnp.int32(0)
    for s in range(SEQS):
        for j in range(BLOCKS):
            hit = owners[s, j] == holder
            slots[jnp.where(hit, jnp.minimum(count, CAP), CAP)] = places[s, j]
            count = count + hit.astype(jnp.int32)
    for c in new_copies:
        c.wait()
    low = pl.ds(pl.multiple_of(xl * 64 + core * 16, 16), 16)
    high = pl.ds(pl.multiple_of(xl * 64 + 32 + core * 16, 16), 16)
    for s in range(SEQS):
        nrope[s] = nrope_t[s].T
        new_part[s, 0:64, :] = nlat[s, :, 0:LANES]
        new_part[s, 64:128, :] = nlat[s, :, LANES : 2 * LANES]
        new_part[s, 128:144, :] = jnp.concatenate([nrope[s, low, :], nrope[s, high, :]], axis=1)
    out_copies = [
        pltpu.make_async_copy(new_part, out.at[x, :, pl.ds(NEW_AT, NEW_ROWS), :], out_sems.at[x])
        for x in range(4)
    ]
    for c in out_copies:
        c.start()
    for c in pool_copies:
        c.wait()
    blocks = [slots[r] for r in range(CAP)]
    for r in range(CAP):
        for x in range(4):
            cached_part[x, r * PIECE : (r + 1) * PIECE, :] = lat[blocks[r], x * PIECE : (x + 1) * PIECE, :]
    for s in range(SEQS):
        c = pltpu.make_async_copy(
            cached_part.at[:, pl.ds(0, LAT_ROWS), :], out.at[:, s, pl.ds(0, LAT_ROWS), :], out_sems.at[4 + s]
        )
        c.start()
        out_copies.append(c)
    for m in range((CAP + 3) // 4):
        quarter = []
        for r in range(4 * m, 4 * m + 4):
            whole = rope[blocks[min(r, CAP - 1)]]
            quarter.append(jnp.where(core == 0, whole[:, 0:32], whole[:, 32:64]))
        both = jnp.concatenate(quarter, axis=1)
        for x in range(4):
            cached_part[x, LAT_ROWS + m * PIECE : LAT_ROWS + (m + 1) * PIECE, :] = both[
                x * PIECE : (x + 1) * PIECE, :
            ]
    for s in range(SEQS):
        c = pltpu.make_async_copy(
            cached_part.at[:, pl.ds(LAT_ROWS, ROPE_ROWS), :],
            out.at[:, s, pl.ds(LAT_ROWS, ROPE_ROWS), :],
            out_sems.at[8 + s],
        )
        c.start()
        out_copies.append(c)
    for c in out_copies:
        c.wait()


def select_kernel(owner, recv, out, new_out, counts, cached, picked, packed, sems, out_sems):
    zp, seq = coords("zp", "y")
    arrive = pltpu.make_async_copy(recv.at[:, pl.ds(0, NEW_AT), :], cached, sems.at[0])
    arrive.start()
    new_copy = pltpu.make_async_copy(
        recv.at[:, pl.ds(NEW_AT, NEW_ROWS), :], new_out, sems.at[1]
    )
    new_copy.start()
    for h in range(16):
        counts[h] = 0

    def scan(s, carry):
        for j in range(BLOCKS):
            h = owner[s, j]
            counts[h] = counts[h] + 1
        return carry

    lax.fori_loop(0, seq, scan, jnp.int32(0))
    ranks, sources = [], []
    for j in range(BLOCKS):
        h = owner[seq, j]
        rank = counts[h]
        counts[h] = rank + 1
        ranks.append(jnp.minimum(rank, CAP - 1))
        sources.append((h & 3) * 4 + (h >> 2))
    arrive.wait()
    for j in range(BLOCKS):
        rows = pl.ds(pl.multiple_of(ranks[j] * PIECE, PIECE), PIECE)
        picked[j * PIECE : (j + 1) * PIECE, :] = cached[sources[j], rows, :]

    def rotary(j):
        rows = pl.ds(pl.multiple_of(LAT_ROWS + (ranks[j] >> 2) * PIECE, PIECE), PIECE)
        tile = cached[sources[j], rows, :]
        odd = (ranks[j] & 1) == 1
        left = jnp.where(odd, tile[:, 32:64], tile[:, 0:32])
        right = jnp.where(odd, tile[:, 96:128], tile[:, 64:96])
        return jnp.where((ranks[j] & 2) == 2, right, left)

    for j in range(BLOCKS // 4):
        packed[j * PIECE : (j + 1) * PIECE, :] = jnp.concatenate(
            [rotary(j + e * BLOCKS // 4) for e in range(4)], axis=1
        )
    picked[PICK_LAT:PICK_ROWS, :] = packed[pl.ds(pl.multiple_of(zp * PICK_PART, 16), PICK_PART), :]
    out_copies = [pltpu.make_async_copy(picked, out.at[d], out_sems.at[d]) for d in range(8)]
    for c in out_copies:
        c.start()
    for c in out_copies + [new_copy]:
        c.wait()


def dot(a, b):
    return lax.dot_general(a, b, (((1,), (0,)), ((), ())), preferred_element_type=f32)


def dot_t(a, b):
    return lax.dot_general(a, b, (((1,), (1,)), ((), ())), preferred_element_type=f32)


def gather_query(refs, query, sems):
    (y,) = coords("y")
    copies = []
    for k in range(4):
        at = lax.rem(y + 4 - k, 4)
        copies.append(pltpu.make_async_copy(refs[k], query.at[at], sems.at[k]))
    for c in copies:
        c.start()
    return copies


def halves(core):
    return [pl.ds(pl.multiple_of(c * 256, 256), 256) for c in (core, 1 - core)]


def joint_query(query, key_up, core, chunk, joint):
    pad = jnp.zeros((TOK, 64), bf16)
    for h in range(2):
        rows = pl.ds((2 * chunk + h) * TOK, TOK)
        nope = query[chunk, :, h * 128 : (h + 1) * 128]
        pos = query[chunk, :, 256 + h * 64 : 256 + (h + 1) * 64]
        for i, cols in enumerate(halves(core)):
            joint[rows, i * 256 : (i + 1) * 256] = dot(nope, key_up[h, :, cols]).astype(bf16)
        joint[rows, 512:640] = jnp.concatenate([pos, pad], axis=1)
        joint[rows, 640:768] = jnp.concatenate([pad, pos], axis=1)


def load_query(joint, start, count):
    low = joint[start : start + count, 0:640]
    high = jnp.concatenate([joint[start : start + count, 0:512], joint[start : start + count, 640:768]], axis=1)
    return low, high


def project(mixed, value_up, core, h):
    own, other = halves(core)
    return dot(mixed[:, 0:256], value_up[h, own, :]) + dot(mixed[:, 256:512], value_up[h, other, :])


def new_kernel(
    q0, q1, q2, q3, key_up, value_up, own, other, stats_out, part_out, token, query, joint, keys, sems
):
    core, xh = coords("core", "xh")
    query_copies = gather_query((q0, q1, q2, q3), query, sems)
    token[...] = jnp.zeros_like(token)
    for i, (which, ref) in enumerate(((core, own), (1 - core, other))):
        rope_rows = pl.ds(pl.multiple_of(which * 16, 16), 16)
        for y in range(4):
            for part in range(4):
                for half in range(2):
                    for tile in range(2):
                        at = tile * 64 + half * 32
                        col = (2 * i + tile) * LANES
                        keys[y, half, part, :, col : col + LANES] = ref[part // 2, part % 2, y, at : at + 32, :]
                    keys[y, half, part, rope_rows, 512:640] = ref[part // 2, part % 2, y, 128:144, :]
    for c in query_copies:
        c.wait()
    for chunk in range(4):
        joint_query(query, key_up, core, chunk, joint)
    rows = 2 * TOK
    row_tok = lax.broadcasted_iota(jnp.int32, (rows, TOK), 0) % TOK + xh * TOK
    col = lax.broadcasted_iota(jnp.int32, (rows, TOK), 1)
    col_tok = col // 32 * 64 + col % 32
    lane = lax.broadcasted_iota(jnp.int32, (rows, LANES), 1)
    causal = [jnp.where(col_tok + 32 * half <= row_tok, 0.0, NEG).astype(f32) for half in range(2)]
    def score(chunk):
        q = load_query(joint, chunk * rows, rows)
        scores = []
        for part in range(chunk + 1):
            for half in range(2):
                s = dot_t(q[half], keys[part, half].reshape(TOK, 640))
                scores.append(s + causal[half] if part == chunk else s)
        return scores

    def soften(chunk, scores):
        top = functools.reduce(jnp.maximum, [jnp.max(s, -1, keepdims=True) for s in scores])
        expo = [jnp.exp2((s - top) * EXP_SCALE) for s in scores]
        denom = functools.reduce(jnp.add, [jnp.sum(e, -1, keepdims=True) for e in expo])
        stats_out[:, chunk * rows : (chunk + 1) * rows] = jnp.where(lane == 0, top, denom).T[0:8]
        return jnp.concatenate([e.astype(bf16) for e in expo], axis=1), denom

    def finish(chunk, weights, denom):
        total = dot(weights, keys[0 : chunk + 1, :, :, :, 0:512].reshape((chunk + 1) * rows, 512))
        mixed = (total / denom).astype(bf16)
        for h in range(2):
            part_out[chunk, :, h * 128 : (h + 1) * 128] = project(
                mixed[h * TOK : (h + 1) * TOK], value_up, core, h
            )

    order = (3, 2, 1, 0)
    scores = {chunk: score(chunk) for chunk in order}
    softened = {chunk: soften(chunk, scores[chunk]) for chunk in order}
    for chunk in order:
        finish(chunk, *softened[chunk])


def prepare_kernel(q0, q1, q2, q3, key_up, joint, query, sems):
    (core,) = coords("core")
    for c in gather_query((q0, q1, q2, q3), query, sems):
        c.wait()
    pad = jnp.zeros((TOK, 64), bf16)
    for chunk in range(4):
        for h in range(2):
            rows = pl.ds((2 * chunk + h) * TOK, TOK)
            nope = query[chunk, :, h * 128 : (h + 1) * 128]
            pos = query[chunk, :, 256 + h * 64 : 256 + (h + 1) * 64]
            for i, cols in enumerate(halves(core)):
                joint[rows, i * 256 : (i + 1) * 256] = dot(nope, key_up[h, :, cols]).astype(bf16)
            pos = jnp.where(core == 0, pos, jnp.concatenate([pos[:, 32:64], pos[:, 0:32]], axis=1))
            joint[rows, 512:640] = jnp.concatenate([pos, pad], axis=1)


def cached_kernel(cached_len, joint, value_up, own, other, stats, new_part, token, out, keys):
    core, seq = coords("core", "y")
    span = PICK_LAT // 4
    pad = jnp.zeros((span, 64), bf16)
    packed = [
        [
            jnp.concatenate([ref[zp, x % 2, x // 2, PICK_LAT:PICK_ROWS, :] for zp in range(2)], axis=0)
            for ref in (own, other)
        ]
        for x in range(4)
    ]
    rows, count = 4 * TOK, 8 * span

    def assemble(half):
        for e in (2 * half, 2 * half + 1):
            for x in range(4):
                start = (e * 4 + x) * span
                for i, ref in enumerate((own, other)):
                    for zp in range(2):
                        keys[start : start + span, (2 * i + zp) * LANES : (2 * i + zp + 1) * LANES] = ref[
                            zp, x % 2, x // 2, e * span : (e + 1) * span, :
                        ]
                lanes = slice(32 * e, 32 * e + 32)
                keys[start : start + span, 512:640] = jnp.concatenate(
                    [packed[x][0][:, lanes], packed[x][1][:, lanes], pad], axis=1
                )

    length = cached_len[seq]
    index = lax.broadcasted_iota(jnp.int32, (1, 2 * count), 1)
    rest = index % span
    position = (index // (4 * span) * (BLOCKS // 4) + rest // PIECE) * 64
    position = position + index // span % 4 * PIECE + rest % PIECE
    bias = jnp.where(position < length, 0.0, NEG).astype(f32)

    def score(group, half):
        q = joint[group * rows : (group + 1) * rows, :]
        at = slice(half * count, (half + 1) * count)
        return dot_t(q, keys[at, :]) + bias[:, at]

    def soften(group, scores):
        state = jnp.concatenate([stats[:, group * rows : (group + 1) * rows]] * 16, axis=0).T
        before, denom_before = state[:, 0:1], state[:, 1:2]
        top = functools.reduce(jnp.maximum, [before] + [jnp.max(s, -1, keepdims=True) for s in scores])
        factor = jnp.exp2((before - top) * EXP_SCALE) * denom_before
        expo = [jnp.exp2((s - top) * EXP_SCALE) for s in scores]
        denom = functools.reduce(jnp.add, [factor] + [jnp.sum(e, -1, keepdims=True) for e in expo])
        weights = jnp.concatenate([e.astype(bf16) for e in expo], axis=1)
        return weights, denom, factor / denom

    def finish(group, weights, denom, share):
        mixed = (dot(weights, keys[:, 0:512]) / denom).astype(bf16)
        for c in range(2):
            chunk = group * 2 + c
            for h in range(2):
                tok = slice((2 * c + h) * TOK, (2 * c + h + 1) * TOK)
                cols = slice(h * 128, (h + 1) * 128)
                fresh = project(mixed[tok], value_up, core, h)
                out[chunk, :, cols] = (fresh + new_part[chunk, :, cols] * share[tok]).astype(bf16)

    assemble(0)
    first = [score(0, 0)]
    assemble(1)
    first.append(score(0, 1))
    second = [score(1, 0), score(1, 1)]
    first = soften(0, first)
    second = soften(1, second)
    finish(0, *first)
    finish(1, *second)


def smem():
    return pl.BlockSpec(memory_space=pltpu.SMEM)


def vmem():
    return pl.BlockSpec(memory_space=pltpu.VMEM)


def anywhere():
    return pl.BlockSpec(memory_space=pl.ANY)


def params(mib):
    return pltpu.CompilerParams(vmem_limit_bytes=mib * MIB)


def shape(dims, kind=bf16):
    return jax.ShapeDtypeStruct(dims, kind)


def on_device(
    query_nope,
    query_rope,
    key_up,
    value_up,
    new_latent,
    new_rope,
    cache_latent,
    cache_rope,
    block_owner,
    block_slot,
    cached_len,
):
    y = lax.axis_index("y")
    send = pl.pallas_call(
        pack_kernel,
        out_shape=shape((4, SEQS, MSG_ROWS, LANES)),
        in_specs=[anywhere()] * 6,
        out_specs=anywhere(),
        scratch_shapes=[
            pltpu.SMEM((SEQS, BLOCKS), jnp.int32),
            pltpu.SMEM((SEQS, BLOCKS), jnp.int32),
            pltpu.SMEM((16,), jnp.int32),
            pltpu.VMEM((32, 64, LANES), bf16),
            pltpu.VMEM((32, 64, 64), bf16),
            pltpu.VMEM((SEQS, 64, 2 * LANES), bf16),
            pltpu.VMEM((SEQS, 64, TOK), bf16),
            pltpu.VMEM((SEQS, TOK, 64), bf16),
            pltpu.VMEM((4, NEW_AT, LANES), bf16),
            pltpu.VMEM((SEQS, NEW_ROWS, LANES), bf16),
            pltpu.SemaphoreType.DMA((6,)),
            pltpu.SemaphoreType.DMA((12,)),
        ],
        compiler_params=params(63),
        name="pack",
    )(block_owner, block_slot, cache_latent, cache_rope, new_latent, jnp.swapaxes(new_rope, 1, 2))
    send, query_nope, query_rope = lax.optimization_barrier((send, query_nope, query_rope))
    recv = lax.all_to_all(send.reshape(16, MSG_ROWS, LANES), PLANE, 0, 0)
    query = jnp.concatenate([query_nope, query_rope], -1)
    queries = []
    for k in range(4):
        part = lax.dynamic_index_in_dim(query, lax.rem(y + k, 4), 0, keepdims=False)
        if k:
            part = lax.ppermute(part, "y", [(i, (i + k) % 4) for i in range(4)])
        queries.append(part)
    picked, new_own = pl.pallas_call(
        select_kernel,
        out_shape=(shape((8, PICK_ROWS, LANES)), shape((16, NEW_ROWS, LANES))),
        in_specs=[smem(), anywhere()],
        out_specs=(anywhere(), anywhere()),
        scratch_shapes=[
            pltpu.SMEM((16,), jnp.int32),
            pltpu.VMEM((16, NEW_AT, LANES), bf16),
            pltpu.VMEM((PICK_ROWS, LANES), bf16),
            pltpu.VMEM((BLOCKS // 4 * PIECE, LANES), bf16),
            pltpu.SemaphoreType.DMA((2,)),
            pltpu.SemaphoreType.DMA((8,)),
        ],
        compiler_params=params(16),
        name="select",
    )(block_owner, recv)
    picked, new_own, *queries = lax.optimization_barrier((picked, new_own, *queries))
    swap = [(0, 1), (1, 0)]
    new_own = new_own.reshape(2, 2, 4, NEW_ROWS, LANES)
    new_other = lax.ppermute(new_own, "core", swap)
    cache_own = lax.all_to_all(picked, SPREAD, 0, 0).reshape(2, 2, 2, PICK_ROWS, LANES)

    rows = 8 * TOK
    stats, part, token = pl.pallas_call(
        new_kernel,
        out_shape=(
            shape((8, rows), f32),
            shape((4, TOK, 256), f32),
            shape((8, LANES), f32),
        ),
        in_specs=[anywhere()] * 4 + [vmem()] * 4,
        out_specs=(vmem(),) * 3,
        scratch_shapes=[
            pltpu.VMEM((4, TOK, 384), bf16),
            pltpu.VMEM((rows, 768), bf16),
            pltpu.VMEM((4, 2, 4, 32, 640), bf16),
            pltpu.SemaphoreType.DMA((4,)),
        ],
        compiler_params=params(24),
        cost_estimate=pl.CostEstimate(flops=3 * 10**9, bytes_accessed=5 * 10**6, transcendentals=700000),
        name="attend_new",
    )(*queries, key_up, value_up, new_own, new_other)
    cache_own, token, *queries = lax.optimization_barrier((cache_own, token, *queries))
    cache_other = lax.ppermute(cache_own, "core", swap)
    joint = pl.pallas_call(
        prepare_kernel,
        out_shape=shape((rows, 640)),
        in_specs=[anywhere()] * 4 + [vmem()],
        out_specs=vmem(),
        scratch_shapes=[pltpu.VMEM((4, TOK, 384), bf16), pltpu.SemaphoreType.DMA((4,))],
        compiler_params=params(16),
        cost_estimate=pl.CostEstimate(flops=2 * 10**8, bytes_accessed=2 * 10**6, transcendentals=0),
        name="prepare",
    )(*queries, key_up)
    mixed = pl.pallas_call(
        cached_kernel,
        out_shape=shape((4, TOK, 256)),
        in_specs=[smem()] + [vmem()] * 7,
        out_specs=vmem(),
        scratch_shapes=[
            pltpu.VMEM((4 * PICK_LAT, 640), bf16),
        ],
        compiler_params=params(24),
        cost_estimate=pl.CostEstimate(flops=4 * 10**9, bytes_accessed=5 * 10**6, transcendentals=1600000),
        name="attend_cached",
    )(cached_len, joint, value_up, cache_own, cache_other, stats, part, token)
    return lax.all_to_all(mixed, "y", 0, 0)


def solution(mesh):
    fine = Mesh(
        mesh.devices.reshape(4, 2, 8, 2, 2, 2), ("y", "xh", "zh", "zp", "core", "xl")
    )
    ctx = ("y", "xh")
    heads = ("zh", "zp", "core", "xl")
    holders = ("y", "xh", "xl")
    return jax.shard_map(
        on_device,
        mesh=fine,
        in_specs=(
            P(None, ctx, heads),
            P(None, ctx, heads),
            P(heads, None, None),
            P(heads, None, None),
            P(None, ctx, None),
            P(None, ctx, None),
            P(holders, None, None),
            P(holders, None, None),
            P(),
            P(),
            P(),
        ),
        out_specs=P(None, ctx, heads),
        check_vma=False,
    )
```

```python
import functools

import jax
import jax.numpy as jnp
from jax import lax
from jax.experimental import pallas as pl
from jax.experimental.pallas import tpu as pltpu
from jax.sharding import Mesh
from jax.sharding import PartitionSpec as P

NEG = -1e30
LOG2E = 1.4426950408889634
EXP_SCALE = 192.0 ** (-0.5) * LOG2E
HOLDER = ("y", "xh", "xl")
PLANE = ("y", "xl", "xh")
SPREAD = ("zp", "xl", "xh")
CAP = 9
PIECE = 16
LANES = 128
SEQS = 4
BLOCKS = 24
TOK = 128
LAT_ROWS = CAP * PIECE
ROPE_ROWS = (CAP + 3) // 4 * PIECE
NEW_AT = LAT_ROWS + ROPE_ROWS
NEW_ROWS = 2 * 64 + 16
MSG_ROWS = NEW_AT + NEW_ROWS
PICK_LAT = BLOCKS * PIECE
PICK_PART = BLOCKS // 4 * PIECE // 2
PICK_ROWS = PICK_LAT + PICK_PART
MIB = 1024 * 1024
bf16 = jnp.bfloat16
f32 = jnp.float32


def coords(*names):
    return [lax.axis_index(n) for n in names]


def pack_kernel(
    owner,
    slot,
    cache_latent,
    cache_rope,
    new_latent,
    new_rope,
    out,
    owners,
    places,
    slots,
    lat,
    rope,
    nlat,
    nrope_t,
    nrope,
    cached_part,
    new_part,
    sems,
    out_sems,
):
    holder, core, xl, zp = coords(HOLDER, "core", "xl", "zp")
    table_copies = [
        pltpu.make_async_copy(owner, owners, sems.at[4]),
        pltpu.make_async_copy(slot, places, sems.at[5]),
    ]
    for c in table_copies:
        c.start()
    cols = pl.ds(pl.multiple_of((core * 2 + zp) * LANES, LANES), LANES)
    half = pl.ds(pl.multiple_of(core * 2 * LANES, 2 * LANES), 2 * LANES)
    rows = pl.ds(pl.multiple_of(xl * 64, 64), 64)
    new_copies = [
        pltpu.make_async_copy(new_latent.at[:, rows, half], nlat, sems.at[0]),
        pltpu.make_async_copy(new_rope, nrope_t, sems.at[1]),
    ]
    pool_copies = [
        pltpu.make_async_copy(cache_latent.at[:, :, cols], lat, sems.at[2]),
        pltpu.make_async_copy(cache_rope, rope, sems.at[3]),
    ]
    for c in new_copies + pool_copies:
        c.start()
    for r in range(CAP):
        slots[r] = 0
    for c in table_copies:
        c.wait()
    count = jnp.int32(0)
    for s in range(SEQS):
        for j in range(BLOCKS):
            hit = owners[s, j] == holder
            slots[jnp.where(hit, jnp.minimum(count, CAP), CAP)] = places[s, j]
            count = count + hit.astype(jnp.int32)
    for c in new_copies:
        c.wait()
    low = pl.ds(pl.multiple_of(xl * 64 + core * 16, 16), 16)
    high = pl.ds(pl.multiple_of(xl * 64 + 32 + core * 16, 16), 16)
    for s in range(SEQS):
        nrope[s] = nrope_t[s].T
        new_part[s, 0:64, :] = nlat[s, :, 0:LANES]
        new_part[s, 64:128, :] = nlat[s, :, LANES : 2 * LANES]
        new_part[s, 128:144, :] = jnp.concatenate([nrope[s, low, :], nrope[s, high, :]], axis=1)
    out_copies = [
        pltpu.make_async_copy(new_part, out.at[:, x, pl.ds(NEW_AT, NEW_ROWS), :], out_sems.at[x])
        for x in range(4)
    ]
    for c in out_copies:
        c.start()
    for c in pool_copies:
        c.wait()
    blocks = [slots[r] for r in range(CAP)]
    flipped = (0, 2, 1, 3)
    for r in range(CAP):
        for x in range(4):
            cached_part[flipped[x], r * PIECE : (r + 1) * PIECE, :] = lat[blocks[r], x * PIECE : (x + 1) * PIECE, :]
    for s in range(SEQS):
        c = pltpu.make_async_copy(
            cached_part.at[:, pl.ds(0, LAT_ROWS), :], out.at[s, :, pl.ds(0, LAT_ROWS), :], out_sems.at[4 + s]
        )
        c.start()
        out_copies.append(c)
    for m in range((CAP + 3) // 4):
        quarter = []
        for r in range(4 * m, 4 * m + 4):
            whole = rope[blocks[min(r, CAP - 1)]]
            quarter.append(jnp.where(core == 0, whole[:, 0:32], whole[:, 32:64]))
        both = jnp.concatenate(quarter, axis=1)
        for x in range(4):
            cached_part[flipped[x], LAT_ROWS + m * PIECE : LAT_ROWS + (m + 1) * PIECE, :] = both[
                x * PIECE : (x + 1) * PIECE, :
            ]
    for s in range(SEQS):
        c = pltpu.make_async_copy(
            cached_part.at[:, pl.ds(LAT_ROWS, ROPE_ROWS), :],
            out.at[s, :, pl.ds(LAT_ROWS, ROPE_ROWS), :],
            out_sems.at[8 + s],
        )
        c.start()
        out_copies.append(c)
    for c in out_copies:
        c.wait()


def select_kernel(owner, recv, out, new_out, counts, cached, picked, packed, sems, out_sems):
    zp, seq = coords("zp", "y")
    arrive = pltpu.make_async_copy(recv.at[:, pl.ds(0, NEW_AT), :], cached, sems.at[0])
    arrive.start()
    new_copy = pltpu.make_async_copy(
        recv.at[:, pl.ds(NEW_AT, NEW_ROWS), :], new_out, sems.at[1]
    )
    new_copy.start()
    for h in range(16):
        counts[h] = 0

    def scan(s, carry):
        for j in range(BLOCKS):
            h = owner[s, j]
            counts[h] = counts[h] + 1
        return carry

    lax.fori_loop(0, seq, scan, jnp.int32(0))
    ranks, sources = [], []
    for j in range(BLOCKS):
        h = owner[seq, j]
        rank = counts[h]
        counts[h] = rank + 1
        ranks.append(jnp.minimum(rank, CAP - 1))
        sources.append((h >> 2) * 4 + (h & 1) * 2 + ((h >> 1) & 1))
    arrive.wait()
    for j in range(BLOCKS):
        rows = pl.ds(pl.multiple_of(ranks[j] * PIECE, PIECE), PIECE)
        picked[j * PIECE : (j + 1) * PIECE, :] = cached[sources[j], rows, :]

    def rotary(j):
        rows = pl.ds(pl.multiple_of(LAT_ROWS + (ranks[j] >> 2) * PIECE, PIECE), PIECE)
        tile = cached[sources[j], rows, :]
        odd = (ranks[j] & 1) == 1
        left = jnp.where(odd, tile[:, 32:64], tile[:, 0:32])
        right = jnp.where(odd, tile[:, 96:128], tile[:, 64:96])
        return jnp.where((ranks[j] & 2) == 2, right, left)

    for j in range(BLOCKS // 4):
        packed[j * PIECE : (j + 1) * PIECE, :] = jnp.concatenate(
            [rotary(j + e * BLOCKS // 4) for e in range(4)], axis=1
        )
    picked[PICK_LAT:PICK_ROWS, :] = packed[pl.ds(pl.multiple_of(zp * PICK_PART, 16), PICK_PART), :]
    out_copies = [pltpu.make_async_copy(picked, out.at[d], out_sems.at[d]) for d in range(8)]
    for c in out_copies:
        c.start()
    for c in out_copies + [new_copy]:
        c.wait()


def dot(a, b):
    return lax.dot_general(a, b, (((1,), (0,)), ((), ())), preferred_element_type=f32)


def dot_t(a, b):
    return lax.dot_general(a, b, (((1,), (1,)), ((), ())), preferred_element_type=f32)


def gather_query(refs, query, sems):
    (y,) = coords("y")
    copies = []
    for k in range(4):
        at = lax.rem(y + 4 - k, 4)
        copies.append(pltpu.make_async_copy(refs[k], query.at[at], sems.at[k]))
    for c in copies:
        c.start()
    return copies


def halves(core):
    return [pl.ds(pl.multiple_of(c * 256, 256), 256) for c in (core, 1 - core)]


def joint_query(query, key_up, core, chunk, joint):
    pad = jnp.zeros((TOK, 64), bf16)
    for h in range(2):
        rows = pl.ds((2 * chunk + h) * TOK, TOK)
        nope = query[chunk, :, h * 128 : (h + 1) * 128]
        pos = query[chunk, :, 256 + h * 64 : 256 + (h + 1) * 64]
        for i, cols in enumerate(halves(core)):
            joint[rows, i * 256 : (i + 1) * 256] = dot(nope, key_up[h, :, cols]).astype(bf16)
        joint[rows, 512:640] = jnp.concatenate([pos, pad], axis=1)
        joint[rows, 640:768] = jnp.concatenate([pad, pos], axis=1)


def load_query(joint, start, count):
    low = joint[start : start + count, 0:640]
    high = jnp.concatenate([joint[start : start + count, 0:512], joint[start : start + count, 640:768]], axis=1)
    return low, high


def project(mixed, value_up, core, h):
    own, other = halves(core)
    return dot(mixed[:, 0:256], value_up[h, own, :]) + dot(mixed[:, 256:512], value_up[h, other, :])


def new_kernel(
    q0, q1, q2, q3, key_up, value_up, own, other, stats_out, part_out, token, query, joint, keys, sems
):
    core, xh = coords("core", "xh")
    query_copies = gather_query((q0, q1, q2, q3), query, sems)
    token[...] = jnp.zeros_like(token)
    for i, (which, ref) in enumerate(((core, own), (1 - core, other))):
        rope_rows = pl.ds(pl.multiple_of(which * 16, 16), 16)
        for y in range(4):
            for part in range(4):
                for half in range(2):
                    for tile in range(2):
                        at = tile * 64 + half * 32
                        col = (2 * i + tile) * LANES
                        keys[y, half, part, :, col : col + LANES] = ref[y, part % 2, part // 2, at : at + 32, :]
                    keys[y, half, part, rope_rows, 512:640] = ref[y, part % 2, part // 2, 128:144, :]
    for c in query_copies:
        c.wait()
    for chunk in range(4):
        joint_query(query, key_up, core, chunk, joint)
    rows = 2 * TOK
    row_tok = lax.broadcasted_iota(jnp.int32, (rows, TOK), 0) % TOK + xh * TOK
    col = lax.broadcasted_iota(jnp.int32, (rows, TOK), 1)
    col_tok = col // 32 * 64 + col % 32
    lane = lax.broadcasted_iota(jnp.int32, (rows, LANES), 1)
    causal = [jnp.where(col_tok + 32 * half <= row_tok, 0.0, NEG).astype(f32) for half in range(2)]
    def score(chunk):
        q = load_query(joint, chunk * rows, rows)
        scores = []
        for part in range(chunk + 1):
            for half in range(2):
                s = dot_t(q[half], keys[part, half].reshape(TOK, 640))
                scores.append(s + causal[half] if part == chunk else s)
        return scores

    def soften(chunk, scores):
        top = functools.reduce(jnp.maximum, [jnp.max(s, -1, keepdims=True) for s in scores])
        expo = [jnp.exp2((s - top) * EXP_SCALE) for s in scores]
        denom = functools.reduce(jnp.add, [jnp.sum(e, -1, keepdims=True) for e in expo])
        stats_out[:, chunk * rows : (chunk + 1) * rows] = jnp.where(lane == 0, top, denom).T[0:8]
        return jnp.concatenate([e.astype(bf16) for e in expo], axis=1), denom

    def finish(chunk, weights, denom):
        total = dot(weights, keys[0 : chunk + 1, :, :, :, 0:512].reshape((chunk + 1) * rows, 512))
        mixed = (total / denom).astype(bf16)
        for h in range(2):
            part_out[chunk, :, h * 128 : (h + 1) * 128] = project(
                mixed[h * TOK : (h + 1) * TOK], value_up, core, h
            )

    order = (3, 2, 1, 0)
    scores = {chunk: score(chunk) for chunk in order}
    softened = {chunk: soften(chunk, scores[chunk]) for chunk in order}
    for chunk in order:
        finish(chunk, *softened[chunk])


def prepare_kernel(q0, q1, q2, q3, key_up, joint, query, sems):
    (core,) = coords("core")
    for c in gather_query((q0, q1, q2, q3), query, sems):
        c.wait()
    pad = jnp.zeros((TOK, 64), bf16)
    for chunk in range(4):
        for h in range(2):
            rows = pl.ds((2 * chunk + h) * TOK, TOK)
            nope = query[chunk, :, h * 128 : (h + 1) * 128]
            pos = query[chunk, :, 256 + h * 64 : 256 + (h + 1) * 64]
            for i, cols in enumerate(halves(core)):
                joint[rows, i * 256 : (i + 1) * 256] = dot(nope, key_up[h, :, cols]).astype(bf16)
            pos = jnp.where(core == 0, pos, jnp.concatenate([pos[:, 32:64], pos[:, 0:32]], axis=1))
            joint[rows, 512:640] = jnp.concatenate([pos, pad], axis=1)


def cached_kernel(cached_len, joint, value_up, own, other, stats, new_part, token, out, keys):
    core, seq = coords("core", "y")
    span = PICK_LAT // 4
    pad = jnp.zeros((span, 64), bf16)
    packed = [
        [
            jnp.concatenate([ref[zp, x % 2, x // 2, PICK_LAT:PICK_ROWS, :] for zp in range(2)], axis=0)
            for ref in (own, other)
        ]
        for x in range(4)
    ]
    rows, count = 4 * TOK, 8 * span

    def assemble(half):
        for e in (2 * half, 2 * half + 1):
            for x in range(4):
                start = (e * 4 + x) * span
                for i, ref in enumerate((own, other)):
                    for zp in range(2):
                        keys[start : start + span, (2 * i + zp) * LANES : (2 * i + zp + 1) * LANES] = ref[
                            zp, x % 2, x // 2, e * span : (e + 1) * span, :
                        ]
                lanes = slice(32 * e, 32 * e + 32)
                keys[start : start + span, 512:640] = jnp.concatenate(
                    [packed[x][0][:, lanes], packed[x][1][:, lanes], pad], axis=1
                )

    length = cached_len[seq]
    index = lax.broadcasted_iota(jnp.int32, (1, 2 * count), 1)
    rest = index % span
    position = (index // (4 * span) * (BLOCKS // 4) + rest // PIECE) * 64
    position = position + index // span % 4 * PIECE + rest % PIECE
    bias = jnp.where(position < length, 0.0, NEG).astype(f32)

    def score(group, half):
        q = joint[group * rows : (group + 1) * rows, :]
        at = slice(half * count, (half + 1) * count)
        return dot_t(q, keys[at, :]) + bias[:, at]

    def soften(group, scores):
        state = jnp.concatenate([stats[:, group * rows : (group + 1) * rows]] * 16, axis=0).T
        before, denom_before = state[:, 0:1], state[:, 1:2]
        top = functools.reduce(jnp.maximum, [before] + [jnp.max(s, -1, keepdims=True) for s in scores])
        factor = jnp.exp2((before - top) * EXP_SCALE) * denom_before
        expo = [jnp.exp2((s - top) * EXP_SCALE) for s in scores]
        denom = functools.reduce(jnp.add, [factor] + [jnp.sum(e, -1, keepdims=True) for e in expo])
        weights = jnp.concatenate([e.astype(bf16) for e in expo], axis=1)
        return weights, denom, factor / denom

    def finish(group, weights, denom, share):
        mixed = (dot(weights, keys[:, 0:512]) / denom).astype(bf16)
        for c in range(2):
            chunk = group * 2 + c
            for h in range(2):
                tok = slice((2 * c + h) * TOK, (2 * c + h + 1) * TOK)
                cols = slice(h * 128, (h + 1) * 128)
                fresh = project(mixed[tok], value_up, core, h)
                out[chunk, :, cols] = (fresh + new_part[chunk, :, cols] * share[tok]).astype(bf16)

    assemble(0)
    first = [score(0, 0)]
    assemble(1)
    first.append(score(0, 1))
    second = [score(1, 0), score(1, 1)]
    first = soften(0, first)
    second = soften(1, second)
    finish(0, *first)
    finish(1, *second)


def smem():
    return pl.BlockSpec(memory_space=pltpu.SMEM)


def vmem():
    return pl.BlockSpec(memory_space=pltpu.VMEM)


def anywhere():
    return pl.BlockSpec(memory_space=pl.ANY)


def params(mib):
    return pltpu.CompilerParams(vmem_limit_bytes=mib * MIB)


def shape(dims, kind=bf16):
    return jax.ShapeDtypeStruct(dims, kind)


def on_device(
    query_nope,
    query_rope,
    key_up,
    value_up,
    new_latent,
    new_rope,
    cache_latent,
    cache_rope,
    block_owner,
    block_slot,
    cached_len,
):
    y = lax.axis_index("y")
    send = pl.pallas_call(
        pack_kernel,
        out_shape=shape((SEQS, 4, MSG_ROWS, LANES)),
        in_specs=[anywhere()] * 6,
        out_specs=anywhere(),
        scratch_shapes=[
            pltpu.SMEM((SEQS, BLOCKS), jnp.int32),
            pltpu.SMEM((SEQS, BLOCKS), jnp.int32),
            pltpu.SMEM((16,), jnp.int32),
            pltpu.VMEM((32, 64, LANES), bf16),
            pltpu.VMEM((32, 64, 64), bf16),
            pltpu.VMEM((SEQS, 64, 2 * LANES), bf16),
            pltpu.VMEM((SEQS, 64, TOK), bf16),
            pltpu.VMEM((SEQS, TOK, 64), bf16),
            pltpu.VMEM((4, NEW_AT, LANES), bf16),
            pltpu.VMEM((SEQS, NEW_ROWS, LANES), bf16),
            pltpu.SemaphoreType.DMA((6,)),
            pltpu.SemaphoreType.DMA((12,)),
        ],
        compiler_params=params(63),
        name="pack",
    )(block_owner, block_slot, cache_latent, cache_rope, new_latent, jnp.swapaxes(new_rope, 1, 2))
    send, query_nope, query_rope = lax.optimization_barrier((send, query_nope, query_rope))
    recv = lax.all_to_all(send.reshape(16, MSG_ROWS, LANES), PLANE, 0, 0)
    query = jnp.concatenate([query_nope, query_rope], -1)
    queries = []
    for k in range(4):
        part = lax.dynamic_index_in_dim(query, lax.rem(y + k, 4), 0, keepdims=False)
        if k:
            part = lax.ppermute(part, "y", [(i, (i + k) % 4) for i in range(4)])
        queries.append(part)
    picked, new_own = pl.pallas_call(
        select_kernel,
        out_shape=(shape((8, PICK_ROWS, LANES)), shape((16, NEW_ROWS, LANES))),
        in_specs=[smem(), anywhere()],
        out_specs=(anywhere(), anywhere()),
        scratch_shapes=[
            pltpu.SMEM((16,), jnp.int32),
            pltpu.VMEM((16, NEW_AT, LANES), bf16),
            pltpu.VMEM((PICK_ROWS, LANES), bf16),
            pltpu.VMEM((BLOCKS // 4 * PIECE, LANES), bf16),
            pltpu.SemaphoreType.DMA((2,)),
            pltpu.SemaphoreType.DMA((8,)),
        ],
        compiler_params=params(16),
        name="select",
    )(block_owner, recv)
    picked, new_own, *queries = lax.optimization_barrier((picked, new_own, *queries))
    swap = [(0, 1), (1, 0)]
    new_own = new_own.reshape(4, 2, 2, NEW_ROWS, LANES)
    new_other = lax.ppermute(new_own, "core", swap)
    cache_own = lax.all_to_all(picked, SPREAD, 0, 0).reshape(2, 2, 2, PICK_ROWS, LANES)

    rows = 8 * TOK
    stats, part, token = pl.pallas_call(
        new_kernel,
        out_shape=(
            shape((8, rows), f32),
            shape((4, TOK, 256), f32),
            shape((8, LANES), f32),
        ),
        in_specs=[anywhere()] * 4 + [vmem()] * 4,
        out_specs=(vmem(),) * 3,
        scratch_shapes=[
            pltpu.VMEM((4, TOK, 384), bf16),
            pltpu.VMEM((rows, 768), bf16),
            pltpu.VMEM((4, 2, 4, 32, 640), bf16),
            pltpu.SemaphoreType.DMA((4,)),
        ],
        compiler_params=params(24),
        cost_estimate=pl.CostEstimate(flops=3 * 10**9, bytes_accessed=5 * 10**6, transcendentals=700000),
        name="attend_new",
    )(*queries, key_up, value_up, new_own, new_other)
    cache_own, token, *queries = lax.optimization_barrier((cache_own, token, *queries))
    cache_other = lax.ppermute(cache_own, "core", swap)
    joint = pl.pallas_call(
        prepare_kernel,
        out_shape=shape((rows, 640)),
        in_specs=[anywhere()] * 4 + [vmem()],
        out_specs=vmem(),
        scratch_shapes=[pltpu.VMEM((4, TOK, 384), bf16), pltpu.SemaphoreType.DMA((4,))],
        compiler_params=params(16),
        cost_estimate=pl.CostEstimate(flops=2 * 10**8, bytes_accessed=2 * 10**6, transcendentals=0),
        name="prepare",
    )(*queries, key_up)
    mixed = pl.pallas_call(
        cached_kernel,
        out_shape=shape((4, TOK, 256)),
        in_specs=[smem()] + [vmem()] * 7,
        out_specs=vmem(),
        scratch_shapes=[
            pltpu.VMEM((4 * PICK_LAT, 640), bf16),
        ],
        compiler_params=params(24),
        cost_estimate=pl.CostEstimate(flops=4 * 10**9, bytes_accessed=5 * 10**6, transcendentals=1600000),
        name="attend_cached",
    )(cached_len, joint, value_up, cache_own, cache_other, stats, part, token)
    return lax.all_to_all(mixed, "y", 0, 0)


def solution(mesh):
    fine = Mesh(
        mesh.devices.reshape(4, 2, 8, 2, 2, 2), ("y", "xh", "zh", "zp", "core", "xl")
    )
    ctx = ("y", "xh")
    heads = ("zh", "zp", "core", "xl")
    holders = ("y", "xh", "xl")
    return jax.shard_map(
        on_device,
        mesh=fine,
        in_specs=(
            P(None, ctx, heads),
            P(None, ctx, heads),
            P(heads, None, None),
            P(heads, None, None),
            P(None, ctx, None),
            P(None, ctx, None),
            P(holders, None, None),
            P(holders, None, None),
            P(),
            P(),
            P(),
        ),
        out_specs=P(None, ctx, heads),
        check_vma=False,
    )
```

```python
import functools

import jax
import jax.numpy as jnp
from jax import lax
from jax.experimental import pallas as pl
from jax.experimental.pallas import tpu as pltpu
from jax.sharding import Mesh
from jax.sharding import PartitionSpec as P

NEG = -1e30
LOG2E = 1.4426950408889634
EXP_SCALE = 192.0 ** (-0.5) * LOG2E
HOLDER = ("y", "xh", "xl")
PLANE = ("y", "xl", "xh")
SPREAD = ("zp", "xl", "xh")
CAP = 9
PIECE = 16
LANES = 128
SEQS = 4
BLOCKS = 24
TOK = 128
LAT_ROWS = CAP * PIECE
ROPE_ROWS = (CAP + 3) // 4 * PIECE
NEW_AT = LAT_ROWS + ROPE_ROWS
NEW_ROWS = 2 * 64 + 16
MSG_ROWS = NEW_AT + NEW_ROWS
PICK_LAT = BLOCKS * PIECE
PICK_PART = BLOCKS // 4 * PIECE // 2
PICK_ROWS = PICK_LAT + PICK_PART
MIB = 1024 * 1024
bf16 = jnp.bfloat16
f32 = jnp.float32


def coords(*names):
    return [lax.axis_index(n) for n in names]


def pack_kernel(
    owner,
    slot,
    cache_latent,
    cache_rope,
    new_latent,
    new_rope,
    out,
    owners,
    places,
    slots,
    lat,
    rope,
    nlat,
    nrope_t,
    nrope,
    cached_part,
    new_part,
    sems,
    out_sems,
):
    holder, core, xl, zp = coords(HOLDER, "core", "xl", "zp")
    table_copies = [
        pltpu.make_async_copy(owner, owners, sems.at[4]),
        pltpu.make_async_copy(slot, places, sems.at[5]),
    ]
    for c in table_copies:
        c.start()
    cols = pl.ds(pl.multiple_of((core * 2 + zp) * LANES, LANES), LANES)
    half = pl.ds(pl.multiple_of(core * 2 * LANES, 2 * LANES), 2 * LANES)
    rows = pl.ds(pl.multiple_of(xl * 64, 64), 64)
    new_copies = [
        pltpu.make_async_copy(new_latent.at[:, rows, half], nlat, sems.at[0]),
        pltpu.make_async_copy(new_rope, nrope_t, sems.at[1]),
    ]
    pool_copies = [
        pltpu.make_async_copy(cache_latent.at[:, :, cols], lat, sems.at[2]),
        pltpu.make_async_copy(cache_rope, rope, sems.at[3]),
    ]
    for c in new_copies + pool_copies:
        c.start()
    for r in range(CAP):
        slots[r] = 0
    for c in table_copies:
        c.wait()
    count = jnp.int32(0)
    for s in range(SEQS):
        for j in range(BLOCKS):
            hit = owners[s, j] == holder
            slots[jnp.where(hit, jnp.minimum(count, CAP), CAP)] = places[s, j]
            count = count + hit.astype(jnp.int32)
    for c in new_copies:
        c.wait()
    low = pl.ds(pl.multiple_of(xl * 64 + core * 16, 16), 16)
    high = pl.ds(pl.multiple_of(xl * 64 + 32 + core * 16, 16), 16)
    for s in range(SEQS):
        nrope[s] = nrope_t[s].T
        new_part[s, 0:64, :] = nlat[s, :, 0:LANES]
        new_part[s, 64:128, :] = nlat[s, :, LANES : 2 * LANES]
        new_part[s, 128:144, :] = jnp.concatenate([nrope[s, low, :], nrope[s, high, :]], axis=1)
    out_copies = [
        pltpu.make_async_copy(new_part, out.at[:, x, pl.ds(NEW_AT, NEW_ROWS), :], out_sems.at[x])
        for x in range(4)
    ]
    for c in out_copies:
        c.start()
    for c in pool_copies:
        c.wait()
    blocks = [slots[r] for r in range(CAP)]
    flipped = (0, 2, 1, 3)
    for r in range(CAP):
        for x in range(4):
            cached_part[flipped[x], r * PIECE : (r + 1) * PIECE, :] = lat[blocks[r], x * PIECE : (x + 1) * PIECE, :]
    for s in range(SEQS):
        c = pltpu.make_async_copy(
            cached_part.at[:, pl.ds(0, LAT_ROWS), :], out.at[s, :, pl.ds(0, LAT_ROWS), :], out_sems.at[4 + s]
        )
        c.start()
        out_copies.append(c)
    for m in range((CAP + 3) // 4):
        quarter = []
        for r in range(4 * m, 4 * m + 4):
            whole = rope[blocks[min(r, CAP - 1)]]
            quarter.append(jnp.where(core == 0, whole[:, 0:32], whole[:, 32:64]))
        both = jnp.concatenate(quarter, axis=1)
        for x in range(4):
            cached_part[flipped[x], LAT_ROWS + m * PIECE : LAT_ROWS + (m + 1) * PIECE, :] = both[
                x * PIECE : (x + 1) * PIECE, :
            ]
    for s in range(SEQS):
        c = pltpu.make_async_copy(
            cached_part.at[:, pl.ds(LAT_ROWS, ROPE_ROWS), :],
            out.at[s, :, pl.ds(LAT_ROWS, ROPE_ROWS), :],
            out_sems.at[8 + s],
        )
        c.start()
        out_copies.append(c)
    for c in out_copies:
        c.wait()


def select_kernel(owner, recv, out, new_out, counts, cached, picked, packed, sems, out_sems):
    zp, seq = coords("zp", "y")
    arrive = pltpu.make_async_copy(recv.at[:, pl.ds(0, NEW_AT), :], cached, sems.at[0])
    arrive.start()
    new_copy = pltpu.make_async_copy(
        recv.at[:, pl.ds(NEW_AT, NEW_ROWS), :], new_out, sems.at[1]
    )
    for h in range(16):
        counts[h] = 0

    def scan(s, carry):
        for j in range(BLOCKS):
            h = owner[s, j]
            counts[h] = counts[h] + 1
        return carry

    lax.fori_loop(0, seq, scan, jnp.int32(0))
    ranks, sources = [], []
    for j in range(BLOCKS):
        h = owner[seq, j]
        rank = counts[h]
        counts[h] = rank + 1
        ranks.append(jnp.minimum(rank, CAP - 1))
        sources.append((h >> 2) * 4 + (h & 1) * 2 + ((h >> 1) & 1))
    arrive.wait()
    new_copy.start()
    for j in range(BLOCKS):
        rows = pl.ds(pl.multiple_of(ranks[j] * PIECE, PIECE), PIECE)
        picked[j * PIECE : (j + 1) * PIECE, :] = cached[sources[j], rows, :]

    def rotary(j):
        rows = pl.ds(pl.multiple_of(LAT_ROWS + (ranks[j] >> 2) * PIECE, PIECE), PIECE)
        tile = cached[sources[j], rows, :]
        odd = (ranks[j] & 1) == 1
        left = jnp.where(odd, tile[:, 32:64], tile[:, 0:32])
        right = jnp.where(odd, tile[:, 96:128], tile[:, 64:96])
        return jnp.where((ranks[j] & 2) == 2, right, left)

    for j in range(BLOCKS // 4):
        packed[j * PIECE : (j + 1) * PIECE, :] = jnp.concatenate(
            [rotary(j + e * BLOCKS // 4) for e in range(4)], axis=1
        )
    picked[PICK_LAT:PICK_ROWS, :] = packed[pl.ds(pl.multiple_of(zp * PICK_PART, 16), PICK_PART), :]
    out_copies = [pltpu.make_async_copy(picked, out.at[d], out_sems.at[d]) for d in range(8)]
    for c in out_copies:
        c.start()
    for c in out_copies + [new_copy]:
        c.wait()


def dot(a, b):
    return lax.dot_general(a, b, (((1,), (0,)), ((), ())), preferred_element_type=f32)


def dot_t(a, b):
    return lax.dot_general(a, b, (((1,), (1,)), ((), ())), preferred_element_type=f32)


def gather_query(refs, query, sems):
    (y,) = coords("y")
    copies = []
    for k in range(4):
        at = lax.rem(y + 4 - k, 4)
        copies.append(pltpu.make_async_copy(refs[k], query.at[at], sems.at[k]))
    for c in copies:
        c.start()
    return copies


def halves(core):
    return [pl.ds(pl.multiple_of(c * 256, 256), 256) for c in (core, 1 - core)]


def joint_query(query, key_up, core, chunk, joint):
    pad = jnp.zeros((TOK, 64), bf16)
    for h in range(2):
        rows = pl.ds((2 * chunk + h) * TOK, TOK)
        nope = query[chunk, :, h * 128 : (h + 1) * 128]
        pos = query[chunk, :, 256 + h * 64 : 256 + (h + 1) * 64]
        for i, cols in enumerate(halves(core)):
            joint[rows, i * 256 : (i + 1) * 256] = dot(nope, key_up[h, :, cols]).astype(bf16)
        joint[rows, 512:640] = jnp.concatenate([pos, pad], axis=1)
        joint[rows, 640:768] = jnp.concatenate([pad, pos], axis=1)


def load_query(joint, start, count):
    low = joint[start : start + count, 0:640]
    high = jnp.concatenate([joint[start : start + count, 0:512], joint[start : start + count, 640:768]], axis=1)
    return low, high


def project(mixed, value_up, core, h):
    own, other = halves(core)
    return dot(mixed[:, 0:256], value_up[h, own, :]) + dot(mixed[:, 256:512], value_up[h, other, :])


def new_kernel(
    q0, q1, q2, q3, key_up, value_up, own, other, stats_out, part_out, token, query, joint, keys, sems
):
    core, xh = coords("core", "xh")
    query_copies = gather_query((q0, q1, q2, q3), query, sems)
    token[...] = jnp.zeros_like(token)
    for i, (which, ref) in enumerate(((core, own), (1 - core, other))):
        rope_rows = pl.ds(pl.multiple_of(which * 16, 16), 16)
        for y in range(4):
            for part in range(4):
                for half in range(2):
                    for tile in range(2):
                        at = tile * 64 + half * 32
                        col = (2 * i + tile) * LANES
                        keys[y, half, part, :, col : col + LANES] = ref[y, part % 2, part // 2, at : at + 32, :]
                    keys[y, half, part, rope_rows, 512:640] = ref[y, part % 2, part // 2, 128:144, :]
    for c in query_copies:
        c.wait()
    for chunk in range(4):
        joint_query(query, key_up, core, chunk, joint)
    rows = 2 * TOK
    row_tok = lax.broadcasted_iota(jnp.int32, (rows, TOK), 0) % TOK + xh * TOK
    col = lax.broadcasted_iota(jnp.int32, (rows, TOK), 1)
    col_tok = col // 32 * 64 + col % 32
    lane = lax.broadcasted_iota(jnp.int32, (rows, LANES), 1)
    causal = [jnp.where(col_tok + 32 * half <= row_tok, 0.0, NEG).astype(f32) for half in range(2)]
    def score(chunk):
        q = load_query(joint, chunk * rows, rows)
        scores = []
        for part in range(chunk + 1):
            for half in range(2):
                s = dot_t(q[half], keys[part, half].reshape(TOK, 640))
                scores.append(s + causal[half] if part == chunk else s)
        return scores

    def soften(chunk, scores):
        top = functools.reduce(jnp.maximum, [jnp.max(s, -1, keepdims=True) for s in scores])
        expo = [jnp.exp2((s - top) * EXP_SCALE) for s in scores]
        denom = functools.reduce(jnp.add, [jnp.sum(e, -1, keepdims=True) for e in expo])
        stats_out[:, chunk * rows : (chunk + 1) * rows] = jnp.where(lane == 0, top, denom).T[0:8]
        return jnp.concatenate([e.astype(bf16) for e in expo], axis=1), denom

    def finish(chunk, weights, denom):
        total = dot(weights, keys[0 : chunk + 1, :, :, :, 0:512].reshape((chunk + 1) * rows, 512))
        mixed = (total / denom).astype(bf16)
        for h in range(2):
            part_out[chunk, :, h * 128 : (h + 1) * 128] = project(
                mixed[h * TOK : (h + 1) * TOK], value_up, core, h
            )

    order = (3, 2, 1, 0)
    scores = {chunk: score(chunk) for chunk in order}
    softened = {chunk: soften(chunk, scores[chunk]) for chunk in order}
    for chunk in order:
        finish(chunk, *softened[chunk])


def prepare_kernel(q0, q1, q2, q3, key_up, joint, query, sems):
    (core,) = coords("core")
    for c in gather_query((q0, q1, q2, q3), query, sems):
        c.wait()
    pad = jnp.zeros((TOK, 64), bf16)
    for chunk in range(4):
        for h in range(2):
            rows = pl.ds((2 * chunk + h) * TOK, TOK)
            nope = query[chunk, :, h * 128 : (h + 1) * 128]
            pos = query[chunk, :, 256 + h * 64 : 256 + (h + 1) * 64]
            for i, cols in enumerate(halves(core)):
                joint[rows, i * 256 : (i + 1) * 256] = dot(nope, key_up[h, :, cols]).astype(bf16)
            pos = jnp.where(core == 0, pos, jnp.concatenate([pos[:, 32:64], pos[:, 0:32]], axis=1))
            joint[rows, 512:640] = jnp.concatenate([pos, pad], axis=1)


def cached_kernel(cached_len, joint, value_up, own, other, stats, new_part, token, out, keys):
    core, seq = coords("core", "y")
    span = PICK_LAT // 4
    pad = jnp.zeros((span, 64), bf16)
    packed = [
        [
            jnp.concatenate([ref[zp, x % 2, x // 2, PICK_LAT:PICK_ROWS, :] for zp in range(2)], axis=0)
            for ref in (own, other)
        ]
        for x in range(4)
    ]
    rows, count = 4 * TOK, 8 * span

    def assemble(half):
        for e in (2 * half, 2 * half + 1):
            for x in range(4):
                start = (e * 4 + x) * span
                for i, ref in enumerate((own, other)):
                    for zp in range(2):
                        keys[start : start + span, (2 * i + zp) * LANES : (2 * i + zp + 1) * LANES] = ref[
                            zp, x % 2, x // 2, e * span : (e + 1) * span, :
                        ]
                lanes = slice(32 * e, 32 * e + 32)
                keys[start : start + span, 512:640] = jnp.concatenate(
                    [packed[x][0][:, lanes], packed[x][1][:, lanes], pad], axis=1
                )

    length = cached_len[seq]
    index = lax.broadcasted_iota(jnp.int32, (1, 2 * count), 1)
    rest = index % span
    position = (index // (4 * span) * (BLOCKS // 4) + rest // PIECE) * 64
    position = position + index // span % 4 * PIECE + rest % PIECE
    bias = jnp.where(position < length, 0.0, NEG).astype(f32)

    def score(group, half):
        q = joint[group * rows : (group + 1) * rows, :]
        at = slice(half * count, (half + 1) * count)
        return dot_t(q, keys[at, :]) + bias[:, at]

    def soften(group, scores):
        state = jnp.concatenate([stats[:, group * rows : (group + 1) * rows]] * 16, axis=0).T
        before, denom_before = state[:, 0:1], state[:, 1:2]
        top = functools.reduce(jnp.maximum, [before] + [jnp.max(s, -1, keepdims=True) for s in scores])
        factor = jnp.exp2((before - top) * EXP_SCALE) * denom_before
        expo = [jnp.exp2((s - top) * EXP_SCALE) for s in scores]
        denom = functools.reduce(jnp.add, [factor] + [jnp.sum(e, -1, keepdims=True) for e in expo])
        weights = jnp.concatenate([e.astype(bf16) for e in expo], axis=1)
        return weights, denom, factor / denom

    def finish(group, weights, denom, share):
        mixed = (dot(weights, keys[:, 0:512]) / denom).astype(bf16)
        for c in range(2):
            chunk = group * 2 + c
            for h in range(2):
                tok = slice((2 * c + h) * TOK, (2 * c + h + 1) * TOK)
                cols = slice(h * 128, (h + 1) * 128)
                fresh = project(mixed[tok], value_up, core, h)
                out[chunk, :, cols] = (fresh + new_part[chunk, :, cols] * share[tok]).astype(bf16)

    assemble(0)
    first = [score(0, 0)]
    assemble(1)
    first.append(score(0, 1))
    second = [score(1, 0), score(1, 1)]
    first = soften(0, first)
    second = soften(1, second)
    finish(0, *first)
    finish(1, *second)


def smem():
    return pl.BlockSpec(memory_space=pltpu.SMEM)


def vmem():
    return pl.BlockSpec(memory_space=pltpu.VMEM)


def anywhere():
    return pl.BlockSpec(memory_space=pl.ANY)


def params(mib):
    return pltpu.CompilerParams(vmem_limit_bytes=mib * MIB)


def shape(dims, kind=bf16):
    return jax.ShapeDtypeStruct(dims, kind)


def on_device(
    query_nope,
    query_rope,
    key_up,
    value_up,
    new_latent,
    new_rope,
    cache_latent,
    cache_rope,
    block_owner,
    block_slot,
    cached_len,
):
    y = lax.axis_index("y")
    send = pl.pallas_call(
        pack_kernel,
        out_shape=shape((SEQS, 4, MSG_ROWS, LANES)),
        in_specs=[anywhere()] * 6,
        out_specs=anywhere(),
        scratch_shapes=[
            pltpu.SMEM((SEQS, BLOCKS), jnp.int32),
            pltpu.SMEM((SEQS, BLOCKS), jnp.int32),
            pltpu.SMEM((16,), jnp.int32),
            pltpu.VMEM((32, 64, LANES), bf16),
            pltpu.VMEM((32, 64, 64), bf16),
            pltpu.VMEM((SEQS, 64, 2 * LANES), bf16),
            pltpu.VMEM((SEQS, 64, TOK), bf16),
            pltpu.VMEM((SEQS, TOK, 64), bf16),
            pltpu.VMEM((4, NEW_AT, LANES), bf16),
            pltpu.VMEM((SEQS, NEW_ROWS, LANES), bf16),
            pltpu.SemaphoreType.DMA((6,)),
            pltpu.SemaphoreType.DMA((12,)),
        ],
        compiler_params=params(63),
        name="pack",
    )(block_owner, block_slot, cache_latent, cache_rope, new_latent, jnp.swapaxes(new_rope, 1, 2))
    send, query_nope, query_rope = lax.optimization_barrier((send, query_nope, query_rope))
    recv = lax.all_to_all(send.reshape(16, MSG_ROWS, LANES), PLANE, 0, 0)
    query = jnp.concatenate([query_nope, query_rope], -1)
    queries = []
    for k in range(4):
        part = lax.dynamic_index_in_dim(query, lax.rem(y + k, 4), 0, keepdims=False)
        if k:
            part = lax.ppermute(part, "y", [(i, (i + k) % 4) for i in range(4)])
        queries.append(part)
    picked, new_own = pl.pallas_call(
        select_kernel,
        out_shape=(shape((8, PICK_ROWS, LANES)), shape((16, NEW_ROWS, LANES))),
        in_specs=[smem(), anywhere()],
        out_specs=(anywhere(), anywhere()),
        scratch_shapes=[
            pltpu.SMEM((16,), jnp.int32),
            pltpu.VMEM((16, NEW_AT, LANES), bf16),
            pltpu.VMEM((PICK_ROWS, LANES), bf16),
            pltpu.VMEM((BLOCKS // 4 * PIECE, LANES), bf16),
            pltpu.SemaphoreType.DMA((2,)),
            pltpu.SemaphoreType.DMA((8,)),
        ],
        compiler_params=params(16),
        name="select",
    )(block_owner, recv)
    picked, new_own, *queries = lax.optimization_barrier((picked, new_own, *queries))
    swap = [(0, 1), (1, 0)]
    new_own = new_own.reshape(4, 2, 2, NEW_ROWS, LANES)
    new_other = lax.ppermute(new_own, "core", swap)
    cache_own = lax.all_to_all(picked, SPREAD, 0, 0).reshape(2, 2, 2, PICK_ROWS, LANES)

    rows = 8 * TOK
    stats, part, token = pl.pallas_call(
        new_kernel,
        out_shape=(
            shape((8, rows), f32),
            shape((4, TOK, 256), f32),
            shape((8, LANES), f32),
        ),
        in_specs=[anywhere()] * 4 + [vmem()] * 4,
        out_specs=(vmem(),) * 3,
        scratch_shapes=[
            pltpu.VMEM((4, TOK, 384), bf16),
            pltpu.VMEM((rows, 768), bf16),
            pltpu.VMEM((4, 2, 4, 32, 640), bf16),
            pltpu.SemaphoreType.DMA((4,)),
        ],
        compiler_params=params(24),
        cost_estimate=pl.CostEstimate(flops=3 * 10**9, bytes_accessed=5 * 10**6, transcendentals=700000),
        name="attend_new",
    )(*queries, key_up, value_up, new_own, new_other)
    cache_own, token, *queries = lax.optimization_barrier((cache_own, token, *queries))
    cache_other = lax.ppermute(cache_own, "core", swap)
    joint = pl.pallas_call(
        prepare_kernel,
        out_shape=shape((rows, 640)),
        in_specs=[anywhere()] * 4 + [vmem()],
        out_specs=vmem(),
        scratch_shapes=[pltpu.VMEM((4, TOK, 384), bf16), pltpu.SemaphoreType.DMA((4,))],
        compiler_params=params(16),
        cost_estimate=pl.CostEstimate(flops=2 * 10**8, bytes_accessed=2 * 10**6, transcendentals=0),
        name="prepare",
    )(*queries, key_up)
    mixed = pl.pallas_call(
        cached_kernel,
        out_shape=shape((4, TOK, 256)),
        in_specs=[smem()] + [vmem()] * 7,
        out_specs=vmem(),
        scratch_shapes=[
            pltpu.VMEM((4 * PICK_LAT, 640), bf16),
        ],
        compiler_params=params(24),
        cost_estimate=pl.CostEstimate(flops=4 * 10**9, bytes_accessed=5 * 10**6, transcendentals=1600000),
        name="attend_cached",
    )(cached_len, joint, value_up, cache_own, cache_other, stats, part, token)
    return lax.all_to_all(mixed, "y", 0, 0)


def solution(mesh):
    fine = Mesh(
        mesh.devices.reshape(4, 2, 8, 2, 2, 2), ("y", "xh", "zh", "zp", "core", "xl")
    )
    ctx = ("y", "xh")
    heads = ("zh", "zp", "core", "xl")
    holders = ("y", "xh", "xl")
    return jax.shard_map(
        on_device,
        mesh=fine,
        in_specs=(
            P(None, ctx, heads),
            P(None, ctx, heads),
            P(heads, None, None),
            P(heads, None, None),
            P(None, ctx, None),
            P(None, ctx, None),
            P(holders, None, None),
            P(holders, None, None),
            P(),
            P(),
            P(),
        ),
        out_specs=P(None, ctx, heads),
        check_vma=False,
    )
```
